32 devices in a mesh: seq: 2 (over core), blk: 16 (over z, y, x).
Axes of the slice: x: 2, y: 2, z: 4, core: 2. Of those that a mesh axis runs over, the one named last changes fastest.
Arguments:
- tokens: bfloat16 [4096, 1024], P(('seq', 'blk')), may hold values from -6 to 6
- cotangent: bfloat16 [4096, 1024], P(('seq', 'blk')), may hold values from -6 to 6
- routes: int32 [4096, 2], P(('seq', 'blk')), may hold values from 0 to 7, all different within a row; in each aligned block of 128 rows (0 to 127, 128 to 255, ...) at most 64 rows name the same one
- gate_codes: int32 [4096, 2], P(('seq', 'blk')), may hold values from 1 to 64
- dropout_key: int32 [2], replicated, may hold values from 0 to 1073741823
- w_gate: bfloat16 [16, 1024, 352], P('blk', 'seq'), may hold values from -0.1875 to 0.1875
- w_up: bfloat16 [16, 1024, 352], P('blk', 'seq'), may hold values from -0.1875 to 0.1875
- w_down: bfloat16 [16, 352, 1024], P('blk', None, 'seq'), may hold values from -0.21875 to 0.21875
Outputs:
- layer_out: bfloat16 [4096, 1024], P(('seq', 'blk'))
- tokens_grad: bfloat16 [4096, 1024], P(('seq', 'blk'))
- gate_grad: bfloat16 [16, 1024, 352], P('blk', 'seq')
- up_grad: bfloat16 [16, 1024, 352], P('blk', 'seq')
- down_grad: bfloat16 [16, 352, 1024], P('blk', None, 'seq')
The draws below stay inside these ranges and needn't reach their ends.
Inputs may be any that keep to these rules, and one draw needn't show every extreme that they name: `routes`: each row names 2 different experts; in the 128 rows of one device no expert is named more than 64 times.
All inputs are finite; a program needn't handle non-finite values.
Results may differ from the reference program's by a relative error of at most 0.0095.
Values may be sent and summed in bfloat16 or wider, within the bound.
No kernel may reach another device: no remote copies, remote signals or barrier semaphores. Data moves between devices by JAX's collectives and lax.ppermute only.
A program may use at most 64 MiB of HBM per device.

```python
import math
import jax
import jax.numpy as jnp
import numpy as np
from jax import lax

D = 1024
FF = 704
TOP = 2
TOK_DEV = 128
EXPERTS = 8
CAP = 64
TOK_GROUP = 2048
TOKENS = 4096
N_SEQ = 2
N_BLK = 16


def touch_ends(entries, stream_key, smallest, top_value):
    extent = entries.shape
    index_at = [jax.random.randint(jax.random.fold_in(stream_key, axis), (), 0, extent[axis]) for axis in range(len(extent))]
    entries = entries.at[tuple(index_at)].set(smallest)
    longest = extent.index(max(extent))
    index_at[longest] = (index_at[longest] + 1) % extent[longest]
    return entries.at[tuple(index_at)].set(top_value)


def level_of(stream_key, dims, split, low, largest):
    level = 1.0
    for axis_at, blocks in split:
        steps = jax.random.uniform(jax.random.fold_in(jax.random.fold_in(stream_key, 6), axis_at), (blocks,), jnp.float32, low / len(split), largest / len(split))
        level = level * jnp.repeat(jnp.exp(steps), dims[axis_at] // blocks).reshape((-1,) + (1,) * (len(dims) - 1 - axis_at))
    return level


def routed_block(key, own, number, rows, number_of, top, bound, lean):
    ranking = jax.random.permutation(key, number_of)
    packed, usual = shares(number_of, rows * top, bound, lean, True), shares(number_of, rows * top, bound, lean, False)
    places = jnp.arange(number_of)

    def named(lengths, offset_by):
        used = int((lengths > 0).sum())
        fixed = max(1, used // 4)
        passed = fixed + (places - fixed + offset_by * (used - fixed)) % max(1, number_of - fixed)
        return jnp.zeros((number_of,), jnp.int32).at[ranking[jnp.where(places < fixed, places, passed)]].set(jnp.asarray(lengths, jnp.int32))

    lengths = jnp.where(number % 4 == 0, named(packed, number // 4), named(usual, number - number // 4 - 1))
    mixed = jax.random.permutation(jax.random.fold_in(own, 3), number_of)
    donor, sink = mixed[0:number_of // 2 * 2:2], mixed[1:number_of // 2 * 2:2]
    room = jnp.minimum(lengths[donor] - 1, bound - lengths[sink]) // 2
    room = jnp.where((donor == ranking[0]) | (sink == ranking[0]) | (lengths[sink] == 0), 0, jnp.maximum(room, 0))
    passed = jax.random.randint(jax.random.fold_in(own, 4), (number_of // 2,), 0, 1 << 20) % (room + 1)
    lengths = lengths.at[donor].add(-passed).at[sink].add(passed)
    labels = jnp.searchsorted(jnp.cumsum(lengths), jnp.arange(rows * top), side="right").astype(jnp.int32)
    listing = labels.reshape(top, rows).T
    listing = listing[jax.random.permutation(jax.random.fold_in(own, 1), rows)]
    offset_by = jax.random.randint(jax.random.fold_in(own, 2), (rows, 1), 0, top)
    return jnp.take_along_axis(listing, (jnp.arange(top)[None, :] + offset_by) % top, axis=1)


def shares(amount, total, most, skew, full):
    weights = [(1 << 20) // math.isqrt(grade ** skew) + 1 for grade in range(1, amount + 1)]
    largest = most if full else min(most, max(-(-total // amount), total * weights[0] // sum(weights)))
    least = 1 if total - largest >= amount - 1 else 0
    given, surplus = [largest] + [least] * (amount - 1), total - largest - least * (amount - 1)
    while surplus > 0:
        candidates = [i for i in range(1, amount) if given[i] < largest] or [i for i in range(1, amount) if given[i] < most]
        whole, remaining = sum([weights[i] for i in candidates]), surplus
        for i in candidates:
            extra = min(most - given[i], max(1, remaining * weights[i] // whole), surplus)
            given[i] = given[i] + extra
            surplus = surplus - extra
    return np.array(given)


def bell_draw(key, dims, spread, most, cuts=(), kind=jnp.bfloat16):
    loudness = level_of(key, dims, cuts, -0.22, 0.18) if cuts else 1.0
    result = jax.random.normal(key, dims, jnp.float32) * spread * loudness
    return jnp.minimum(jnp.maximum(result, -most), most).astype(kind)


def setup_inputs(seed: int = 0) -> dict:
    splits = jax.random.split(jax.random.key(seed), 9)
    tokens = bell_draw(splits[0], (TOKENS, D), 1.0, 6.0, ((0, 32),))
    cotangent = bell_draw(splits[1], (TOKENS, D), 1.0, 6.0, ((0, 32),))
    routes_keys = jax.random.split(jax.random.fold_in(splits[2], 1), TOKENS // TOK_DEV)
    routes_turns = jax.random.permutation(jax.random.fold_in(splits[2], 3), TOKENS // TOK_DEV)
    routes = jax.vmap(lambda own, number: routed_block(jax.random.fold_in(splits[2], 2), own, number, TOK_DEV, EXPERTS, TOP, CAP, 2))(routes_keys, routes_turns).reshape((TOKENS, TOP))
    gate_codes = touch_ends(jax.random.randint(splits[3], (TOKENS, TOP), 1, 65), jax.random.fold_in(splits[3], 1), 1, 64).astype(jnp.int32)
    dropout_key = jax.random.randint(splits[4], (2,), 0, 1073741824).astype(jnp.int32)
    w_gate = bell_draw(splits[5], (2 * EXPERTS, D, FF // 2), D ** -0.5, 0.1875, ((0, 16), (1, 2)))
    w_up = bell_draw(splits[6], (2 * EXPERTS, D, FF // 2), D ** -0.5, 0.1875, ((0, 16), (1, 2)))
    w_down = bell_draw(splits[7], (2 * EXPERTS, FF // 2, D), FF ** -0.5, 0.21875, ((0, 16), (2, 2)))
    return {"tokens": tokens, "cotangent": cotangent, "routes": routes, "gate_codes": gate_codes, "dropout_key": dropout_key, "w_gate": w_gate, "w_up": w_up, "w_down": w_down}


mixing_factor = 73244475


def scramble(values):
    values = values ^ ((values >> 16) & 65535)
    values = values * mixing_factor
    values = values ^ ((values >> 16) & 65535)
    values = values * mixing_factor
    return values ^ ((values >> 16) & 65535)


def keep_scale(token_ids, columns, key_pair):
    base_hash = scramble(key_pair[0] ^ scramble(key_pair[1]))
    mixed_ids = scramble(token_ids ^ base_hash)
    hashed = scramble(mixed_ids[:, None] ^ (columns[None, :] * 40503))
    return jnp.where((hashed & 1023) >= 128, jnp.float32(8.0 / 7.0), jnp.float32(0.0))


def reference(tokens, cotangent, routes, gate_codes, dropout_key, w_gate, w_up, w_down):
    expert_count = w_gate.shape[0] // 2
    half_width = w_gate.shape[2]
    hidden_width = 2 * half_width
    model_width = w_gate.shape[1]
    gate_full = w_gate.reshape(expert_count, 2, model_width, half_width).transpose(0, 2, 1, 3).reshape(expert_count, model_width, hidden_width)
    up_full = w_up.reshape(expert_count, 2, model_width, half_width).transpose(0, 2, 1, 3).reshape(expert_count, model_width, hidden_width)
    down_full = w_down.reshape(expert_count, hidden_width, model_width)
    pair_count = TOKENS * TOP
    pair_expert = routes.reshape(-1).astype(jnp.int32)
    pair_token = (jnp.arange(pair_count) // TOP).astype(jnp.int32)
    pair_gate = gate_codes.reshape(-1).astype(jnp.float32) / 64.0
    pair_group = pair_token // TOK_GROUP
    segment_key = pair_expert * N_SEQ + pair_group
    sorted_order = jnp.argsort(segment_key, stable=True).astype(jnp.int32)
    segment_total = expert_count * N_SEQ
    seg_counts = jax.ops.segment_sum(jnp.ones(pair_count, jnp.int32), segment_key, num_segments=segment_total)
    seg_starts = jnp.cumsum(seg_counts) - seg_counts
    seg_length = N_BLK * CAP
    positions = jnp.arange(seg_length, dtype=jnp.int32)
    valid_slot = positions[None, :] < seg_counts[:, None]
    clipped = jnp.clip(seg_starts[:, None] + positions[None, :], 0, pair_count - 1).astype(jnp.int32)
    slot_pairs = jnp.where(valid_slot, sorted_order[clipped], 0)
    key_pair = dropout_key.astype(jnp.int32)

    def per_expert(carried, expert):
        out_acc, grad_acc = carried
        gate_mat = gate_full[expert]
        up_mat = up_full[expert]
        down_mat = down_full[expert]
        columns = expert * hidden_width + jnp.arange(hidden_width, dtype=jnp.int32)
        sums_gate = jnp.zeros((model_width, hidden_width), jnp.float32)
        sums_up = jnp.zeros((model_width, hidden_width), jnp.float32)
        sums_down = jnp.zeros((hidden_width, model_width), jnp.float32)
        for group_index in range(N_SEQ):
            chosen = slot_pairs[expert * N_SEQ + group_index]
            live_slot = valid_slot[expert * N_SEQ + group_index]
            token_of = pair_token[chosen]
            weight_of = jnp.where(live_slot, pair_gate[chosen], 0.0)
            inputs = tokens[token_of] * live_slot[:, None].astype(tokens.dtype)
            drop_scale = keep_scale(token_of, columns, key_pair)
            gate_pre = jnp.dot(inputs, gate_mat, preferred_element_type=jnp.float32)
            up_pre = jnp.dot(inputs, up_mat, preferred_element_type=jnp.float32)
            sigmoid_gate = jax.nn.sigmoid(gate_pre)
            silu_gate = gate_pre * sigmoid_gate
            hidden = (silu_gate * up_pre * drop_scale).astype(jnp.bfloat16)
            expert_out = jnp.dot(hidden, down_mat, preferred_element_type=jnp.float32)
            slot_cot = (weight_of[:, None] * cotangent[token_of].astype(jnp.float32)).astype(jnp.bfloat16)
            hidden_grad = jnp.dot(slot_cot, down_mat.T, preferred_element_type=jnp.float32) * drop_scale
            gate_pre_grad = (hidden_grad * up_pre * sigmoid_gate * (1.0 + gate_pre * (1.0 - sigmoid_gate))).astype(jnp.bfloat16)
            up_pre_grad = (hidden_grad * silu_gate).astype(jnp.bfloat16)
            input_grad = jnp.dot(gate_pre_grad, gate_mat.T, preferred_element_type=jnp.float32) + jnp.dot(up_pre_grad, up_mat.T, preferred_element_type=jnp.float32)
            out_acc = out_acc.at[token_of].add(weight_of[:, None] * expert_out)
            grad_acc = grad_acc.at[token_of].add(jnp.where(live_slot[:, None], input_grad, 0.0))
            piece_gate = jnp.dot(inputs.T, gate_pre_grad, preferred_element_type=jnp.float32)
            piece_up = jnp.dot(inputs.T, up_pre_grad, preferred_element_type=jnp.float32)
            piece_down = jnp.dot(hidden.T, slot_cot, preferred_element_type=jnp.float32)
            sums_gate = sums_gate + lax.optimization_barrier(piece_gate.astype(jnp.bfloat16)).astype(jnp.float32)
            sums_up = sums_up + lax.optimization_barrier(piece_up.astype(jnp.bfloat16)).astype(jnp.float32)
            sums_down = sums_down + lax.optimization_barrier(piece_down.astype(jnp.bfloat16)).astype(jnp.float32)
        return (out_acc, grad_acc), (sums_gate.astype(jnp.bfloat16), sums_up.astype(jnp.bfloat16), sums_down.astype(jnp.bfloat16))

    start_acc = (jnp.zeros((TOKENS, model_width), jnp.float32), jnp.zeros((TOKENS, model_width), jnp.float32))
    finals, stacked = lax.scan(per_expert, start_acc, jnp.arange(expert_count, dtype=jnp.int32))
    gate_grad = stacked[0].reshape(expert_count, model_width, 2, half_width).transpose(0, 2, 1, 3).reshape(2 * expert_count, model_width, half_width)
    up_grad = stacked[1].reshape(expert_count, model_width, 2, half_width).transpose(0, 2, 1, 3).reshape(2 * expert_count, model_width, half_width)
    down_grad = stacked[2].reshape(2 * expert_count, half_width, model_width)
    return (finals[0].astype(jnp.bfloat16), finals[1].astype(jnp.bfloat16), gate_grad, up_grad, down_grad)
```

```python
import jax
import jax.numpy as jnp
from jax import lax
from jax.sharding import PartitionSpec as P

mixing_factor = 73244475
contract_last = (((1,), (1,)), ((), ()))
contract_first = (((0,), (0,)), ((), ()))


def scramble(values):
    values = values ^ values >> 16 & 65535
    values = values * mixing_factor
    values = values ^ values >> 16 & 65535
    values = values * mixing_factor
    return values ^ values >> 16 & 65535


def keep_scale(token_ids, columns, key_pair):
    base_hash = scramble(key_pair[0] ^ scramble(key_pair[1]))
    mixed_ids = scramble(token_ids ^ base_hash)
    hashed = scramble(mixed_ids[:, None] ^ columns[None, :] * 40503)
    return jnp.where(hashed & 1023 >= 128, jnp.float32(8.0 / 7.0), jnp.float32(0.0))


def flipped(values, axis, mask):
    return lax.ppermute(values, axis, [(i, i ^ mask) for i in range(lax.axis_size(axis))])


def local(tokens, cotangent, routes, gate_codes, dropout_key, w_gate, w_up, w_down):
    seq_count = lax.axis_size("seq")
    block_count = lax.axis_size("blk")
    seq_index = lax.axis_index("seq")
    blk_index = lax.axis_index("blk")
    tok_rows, model_width = tokens.shape
    top_count = routes.shape[1]
    expert_count = block_count // 2
    capacity = 2 * tok_rows * top_count // expert_count
    half_width = w_gate.shape[2]
    part_width = w_gate.shape[1]
    planes = 1 << (block_count.bit_length() // 2)
    plane_experts = expert_count // planes
    plane_stride = 2 * plane_experts
    parity = blk_index % 2
    expert_here = blk_index // 2

    table = jnp.concatenate([routes.T, gate_codes.T], axis=0)
    tables = lax.all_gather(table, "blk")

    own_weights = jnp.stack([w_gate[0].T, w_up[0].T, w_down[0]])
    pair_weights = flipped(own_weights, "blk", 1)

    def spread(part):
        chunks = {0: part}
        step = planes // 2
        while step:
            for place in sorted(chunks):
                chunks[place ^ step] = flipped(chunks[place], "blk", step * plane_stride)
            step //= 2
        return [chunks[place] for place in range(planes)]

    token_chunks = spread(tokens)
    cot_chunks = spread(cotangent)

    def table_of(column, place):
        source = blk_index ^ (place * plane_stride + column * 2)
        return lax.dynamic_index_in_dim(tables, source, 0, keepdims=False), source

    earlier = (
        jnp.arange(tok_rows)[:, None] < jnp.arange(tok_rows)[None, :]
    ).astype(jnp.bfloat16)

    def placed(table_rows, expert):
        hits = [table_rows[:, k] == expert for k in range(top_count)]
        named = hits[0]
        for hit in hits[1:]:
            named = named | hit
        rank = jnp.dot(
            named.astype(jnp.bfloat16), earlier, preferred_element_type=jnp.float32
        ).astype(jnp.int32)
        slots = jnp.arange(capacity, dtype=jnp.int32)
        chosen = named[:, None, :] & (rank[:, None, :] == slots[None, :, None])
        gates = jnp.zeros(table_rows[:, 0].shape, jnp.float32)
        for k in range(top_count):
            gates = gates + jnp.where(hits[k], table_rows[:, top_count + k], 0).astype(jnp.float32)
        return chosen, gates / 64.0

    column_tables = []
    column_sources = []
    for column in range(plane_experts):
        picked = [table_of(column, place) for place in range(planes)]
        column_tables.append(jnp.stack([entry[0] for entry in picked]))
        column_sources.append(jnp.stack([entry[1] for entry in picked]))

    select = []
    weigh = []
    for column in range(plane_experts):
        chosen, gates = placed(column_tables[0], expert_here ^ column)
        select.append(chosen.astype(jnp.bfloat16))
        weigh.append(jnp.where(chosen, gates[:, None, :], 0.0).astype(jnp.bfloat16))

    token_ids = []
    for column in range(plane_experts):
        chosen, _ = placed(column_tables[column], expert_here)
        within = jnp.sum(
            jnp.where(chosen, jnp.arange(tok_rows, dtype=jnp.int32)[None, None, :], 0), axis=2
        )
        first = (seq_index * block_count + column_sources[column]) * tok_rows
        token_ids.append((within + first[:, None]).reshape(-1))
    token_ids = jnp.concatenate(token_ids)

    def compact(choice, chunks):
        return jnp.concatenate(
            [
                jnp.dot(choice[place], chunks[place], preferred_element_type=jnp.float32).astype(
                    jnp.bfloat16
                )
                for place in range(planes)
            ]
        )

    def gathered(choices, chunks):
        sent = [
            flipped(compact(choices[column], chunks), "blk", 2 * column)
            for column in range(1, plane_experts)
        ]
        return jnp.concatenate([compact(choices[0], chunks)] + sent)

    rows_in = gathered(select, token_chunks)
    rows_cot = gathered(weigh, cot_chunks)

    weights = lax.all_gather(
        jnp.stack([own_weights, pair_weights], axis=1), "seq", axis=3, tiled=True
    ).reshape(3, 2 * half_width, model_width)
    gate_mat, up_mat, down_mat = weights[0], weights[1], weights[2]

    unit = jnp.arange(half_width, dtype=jnp.int32)
    columns = expert_here * (2 * half_width) + jnp.concatenate(
        [parity * half_width + unit, (1 - parity) * half_width + unit]
    )
    drop_scale = keep_scale(token_ids, columns, dropout_key)
    gate_pre = lax.dot_general(rows_in, gate_mat, contract_last, preferred_element_type=jnp.float32)
    up_pre = lax.dot_general(rows_in, up_mat, contract_last, preferred_element_type=jnp.float32)
    sigmoid_gate = jax.nn.sigmoid(gate_pre)
    silu_gate = gate_pre * sigmoid_gate
    hidden = (silu_gate * up_pre * drop_scale).astype(jnp.bfloat16)
    expert_out = jnp.dot(hidden, down_mat, preferred_element_type=jnp.float32)
    hidden_grad = (
        lax.dot_general(rows_cot, down_mat, contract_last, preferred_element_type=jnp.float32)
        * drop_scale
    )
    gate_pre_grad = (
        hidden_grad * up_pre * sigmoid_gate * (1.0 + gate_pre * (1.0 - sigmoid_gate))
    ).astype(jnp.bfloat16)
    up_pre_grad = (hidden_grad * silu_gate).astype(jnp.bfloat16)
    input_grad = jnp.dot(gate_pre_grad, gate_mat, preferred_element_type=jnp.float32) + jnp.dot(
        up_pre_grad, up_mat, preferred_element_type=jnp.float32
    )

    def brought_back(slot_rows, choices):
        slot_rows = slot_rows.astype(jnp.bfloat16).reshape(
            plane_experts, planes, capacity, model_width
        )
        blocks = [slot_rows[0]] + [
            flipped(slot_rows[column], "blk", 2 * column) for column in range(1, plane_experts)
        ]
        sums = {}
        for place in range(planes):
            choice = jnp.concatenate([choices[column][place] for column in range(plane_experts)])
            block = jnp.concatenate([blocks[column][place] for column in range(plane_experts)])
            sums[place] = lax.dot_general(
                choice, block, contract_first, preferred_element_type=jnp.float32
            )
        step = 1
        while step < planes:
            for place in sorted(sums, reverse=True):
                if place & step:
                    sums[place ^ step] = sums[place ^ step] + flipped(
                        sums[place].astype(jnp.bfloat16), "blk", step * plane_stride
                    ).astype(jnp.float32)
                    del sums[place]
            step *= 2
        return sums[0].astype(jnp.bfloat16)

    layer_out = brought_back(expert_out, weigh)
    tokens_grad = brought_back(input_grad, select)

    def part_sums(target):
        width = part_width
        inputs_part = lax.dynamic_slice_in_dim(rows_in, target * width, width, 1)
        cot_part = lax.dynamic_slice_in_dim(rows_cot, target * width, width, 1)
        return jnp.stack(
            [
                lax.dot_general(left, right, contract_first, preferred_element_type=jnp.float32)
                for left, right in (
                    (gate_pre_grad, inputs_part),
                    (up_pre_grad, inputs_part),
                    (hidden, cot_part),
                )
            ]
        )

    arrived = [
        lax.ppermute(
            part_sums((seq_index + shift) % seq_count).astype(jnp.bfloat16),
            "seq",
            [(i, (i + shift) % seq_count) for i in range(seq_count)],
        ).astype(jnp.float32)
        for shift in range(1, seq_count)
    ]
    totals = part_sums(seq_index)
    for part in arrived:
        totals = totals + part
    totals = totals.reshape(3, 2, half_width, part_width)
    grads = totals[:, 0] + flipped(totals[:, 1].astype(jnp.bfloat16), "blk", 1).astype(jnp.float32)
    grads = grads.astype(jnp.bfloat16)
    return (layer_out, tokens_grad, grads[0].T[None], grads[1].T[None], grads[2][None])


def solution(mesh):
    placed = (
        P(("seq", "blk"), None),
        P(("seq", "blk"), None),
        P(("seq", "blk"), None),
        P(("seq", "blk"), None),
        P(),
        P("blk", "seq", None),
        P("blk", "seq", None),
        P("blk", None, "seq"),
    )
    return jax.shard_map(
        local,
        mesh=mesh,
        in_specs=placed,
        out_specs=(
            P(("seq", "blk"), None),
            P(("seq", "blk"), None),
            P("blk", "seq", None),
            P("blk", "seq", None),
            P("blk", None, "seq"),
        ),
        check_vma=False,
    )
```

```python
import jax
import jax.numpy as jnp
from jax import lax
from jax.sharding import PartitionSpec as P

mixing_factor = 73244475
contract_last = (((1,), (1,)), ((), ()))
contract_first = (((0,), (0,)), ((), ()))


def scramble(values):
    values = values ^ values >> 16 & 65535
    values = values * mixing_factor
    values = values ^ values >> 16 & 65535
    values = values * mixing_factor
    return values ^ values >> 16 & 65535


def keep_scale(token_ids, columns, key_pair):
    base_hash = scramble(key_pair[0] ^ scramble(key_pair[1]))
    mixed_ids = scramble(token_ids ^ base_hash)
    hashed = scramble(mixed_ids[:, None] ^ columns[None, :] * 40503)
    return jnp.where(hashed & 1023 >= 128, jnp.float32(8.0 / 7.0), jnp.float32(0.0))


def flipped(values, axis, mask):
    return lax.ppermute(values, axis, [(i, i ^ mask) for i in range(lax.axis_size(axis))])


def local(tokens, cotangent, routes, gate_codes, dropout_key, w_gate, w_up, w_down):
    seq_count = lax.axis_size("seq")
    block_count = lax.axis_size("blk")
    seq_index = lax.axis_index("seq")
    blk_index = lax.axis_index("blk")
    tok_rows, model_width = tokens.shape
    top_count = routes.shape[1]
    expert_count = block_count // 2
    capacity = 2 * tok_rows * top_count // expert_count
    half_width = w_gate.shape[2]
    part_width = w_gate.shape[1]
    planes = 1 << (block_count.bit_length() // 2)
    plane_experts = expert_count // planes
    plane_stride = 2 * plane_experts
    parity = blk_index % 2
    expert_here = blk_index // 2

    tables = jnp.concatenate([routes.T, gate_codes.T], axis=0)[None]
    step = planes // 2
    while step:
        tables = jnp.stack([tables, flipped(tables, "blk", step * plane_stride)], axis=1)
        tables = tables.reshape((-1,) + tables.shape[2:])
        step //= 2
    tables = jnp.stack(
        [tables]
        + [flipped(tables, "blk", 2 * column) for column in range(1, plane_experts)]
    )

    own_weights = jnp.stack([w_gate[0].T, w_up[0].T, w_down[0]])
    pair_weights = flipped(own_weights, "blk", 1)

    def widened(part):
        parts = [part] + [
            lax.ppermute(
                part, "seq", [(i, (i - shift) % seq_count) for i in range(seq_count)]
            )
            for shift in range(1, seq_count)
        ]
        return jnp.concatenate(
            [
                lax.select_n(
                    (place - seq_index) % seq_count == 1, *parts
                )
                if seq_count == 2
                else lax.switch(
                    (place - seq_index) % seq_count, [lambda p=p: p for p in parts]
                )
                for place in range(seq_count)
            ],
            axis=2,
        )

    def spread(part):
        chunks = {0: part}
        step = planes // 2
        while step:
            for place in sorted(chunks):
                chunks[place ^ step] = flipped(chunks[place], "blk", step * plane_stride)
            step //= 2
        return [chunks[place] for place in range(planes)]

    token_chunks = spread(tokens)
    cot_chunks = spread(cotangent)

    earlier = (
        jnp.arange(tok_rows)[:, None] < jnp.arange(tok_rows)[None, :]
    ).astype(jnp.bfloat16)

    def placed(table_rows, expert):
        hits = [table_rows[:, k] == expert for k in range(top_count)]
        named = hits[0]
        for hit in hits[1:]:
            named = named | hit
        rank = jnp.dot(
            named.astype(jnp.bfloat16), earlier, preferred_element_type=jnp.float32
        ).astype(jnp.int32)
        slots = jnp.arange(capacity, dtype=jnp.int32)
        chosen = named[:, None, :] & (rank[:, None, :] == slots[None, :, None])
        gates = jnp.zeros(table_rows[:, 0].shape, jnp.float32)
        for k in range(top_count):
            gates = gates + jnp.where(hits[k], table_rows[:, top_count + k], 0).astype(jnp.float32)
        return chosen, gates / 64.0

    places = jnp.arange(planes, dtype=jnp.int32) * plane_stride
    column_tables = [tables[column] for column in range(plane_experts)]
    column_sources = [blk_index ^ (places + 2 * column) for column in range(plane_experts)]

    select = []
    weigh = []
    for column in range(plane_experts):
        chosen, gates = placed(column_tables[0], expert_here ^ column)
        select.append(chosen.astype(jnp.bfloat16))
        weigh.append(jnp.where(chosen, gates[:, None, :], 0.0).astype(jnp.bfloat16))

    token_ids = []
    for column in range(plane_experts):
        chosen, _ = placed(column_tables[column], expert_here)
        within = jnp.sum(
            jnp.where(chosen, jnp.arange(tok_rows, dtype=jnp.int32)[None, None, :], 0), axis=2
        )
        first = (seq_index * block_count + column_sources[column]) * tok_rows
        token_ids.append((within + first[:, None]).reshape(-1))
    token_ids = jnp.concatenate(token_ids)

    def compact(choice, chunks):
        return jnp.concatenate(
            [
                jnp.dot(choice[place], chunks[place], preferred_element_type=jnp.float32).astype(
                    jnp.bfloat16
                )
                for place in range(planes)
            ]
        )

    def gathered(choices, chunks):
        sent = [
            flipped(compact(choices[column], chunks), "blk", 2 * column)
            for column in range(1, plane_experts)
        ]
        return jnp.concatenate([compact(choices[0], chunks)] + sent)

    rows_in = gathered(select, token_chunks)
    rows_cot = gathered(weigh, cot_chunks)

    weights = jnp.concatenate([widened(own_weights), widened(pair_weights)], axis=1)
    gate_mat, up_mat, down_mat = weights[0], weights[1], weights[2]

    unit = jnp.arange(half_width, dtype=jnp.int32)
    columns = expert_here * (2 * half_width) + jnp.concatenate(
        [parity * half_width + unit, (1 - parity) * half_width + unit]
    )
    drop_scale = keep_scale(token_ids, columns, dropout_key)
    gate_pre = lax.dot_general(rows_in, gate_mat, contract_last, preferred_element_type=jnp.float32)
    up_pre = lax.dot_general(rows_in, up_mat, contract_last, preferred_element_type=jnp.float32)
    sigmoid_gate = jax.nn.sigmoid(gate_pre)
    silu_gate = gate_pre * sigmoid_gate
    hidden = (silu_gate * up_pre * drop_scale).astype(jnp.bfloat16)
    expert_out = jnp.dot(hidden, down_mat, preferred_element_type=jnp.float32)
    hidden_grad = (
        lax.dot_general(rows_cot, down_mat, contract_last, preferred_element_type=jnp.float32)
        * drop_scale
    )
    gate_pre_grad = (
        hidden_grad * up_pre * sigmoid_gate * (1.0 + gate_pre * (1.0 - sigmoid_gate))
    ).astype(jnp.bfloat16)
    up_pre_grad = (hidden_grad * silu_gate).astype(jnp.bfloat16)
    input_grad = jnp.dot(gate_pre_grad, gate_mat, preferred_element_type=jnp.float32) + jnp.dot(
        up_pre_grad, up_mat, preferred_element_type=jnp.float32
    )

    def brought_back(slot_rows, choices):
        slot_rows = slot_rows.astype(jnp.bfloat16).reshape(
            plane_experts, planes, capacity, model_width
        )
        blocks = [slot_rows[0]] + [
            flipped(slot_rows[column], "blk", 2 * column) for column in range(1, plane_experts)
        ]
        sums = {}
        for place in range(planes):
            choice = jnp.concatenate([choices[column][place] for column in range(plane_experts)])
            block = jnp.concatenate([blocks[column][place] for column in range(plane_experts)])
            sums[place] = lax.dot_general(
                choice, block, contract_first, preferred_element_type=jnp.float32
            )
        step = 1
        while step < planes:
            for place in sorted(sums, reverse=True):
                if place & step:
                    sums[place ^ step] = sums[place ^ step] + flipped(
                        sums[place].astype(jnp.bfloat16), "blk", step * plane_stride
                    ).astype(jnp.float32)
                    del sums[place]
            step *= 2
        return sums[0].astype(jnp.bfloat16)

    layer_out = brought_back(expert_out, weigh)
    tokens_grad = brought_back(input_grad, select)

    def part_sums(target):
        width = part_width
        inputs_part = lax.dynamic_slice_in_dim(rows_in, target * width, width, 1)
        cot_part = lax.dynamic_slice_in_dim(rows_cot, target * width, width, 1)
        return jnp.stack(
            [
                lax.dot_general(left, right, contract_first, preferred_element_type=jnp.float32)
                for left, right in (
                    (gate_pre_grad, inputs_part),
                    (up_pre_grad, inputs_part),
                    (hidden, cot_part),
                )
            ]
        )

    arrived = [
        lax.ppermute(
            part_sums((seq_index + shift) % seq_count).astype(jnp.bfloat16),
            "seq",
            [(i, (i + shift) % seq_count) for i in range(seq_count)],
        ).astype(jnp.float32)
        for shift in range(1, seq_count)
    ]
    totals = part_sums(seq_index)
    for part in arrived:
        totals = totals + part
    totals = totals.reshape(3, 2, half_width, part_width)
    grads = totals[:, 0] + flipped(totals[:, 1].astype(jnp.bfloat16), "blk", 1).astype(jnp.float32)
    grads = grads.astype(jnp.bfloat16)
    return (layer_out, tokens_grad, grads[0].T[None], grads[1].T[None], grads[2][None])


def solution(mesh):
    placed = (
        P(("seq", "blk"), None),
        P(("seq", "blk"), None),
        P(("seq", "blk"), None),
        P(("seq", "blk"), None),
        P(),
        P("blk", "seq", None),
        P("blk", "seq", None),
        P("blk", None, "seq"),
    )
    return jax.shard_map(
        local,
        mesh=mesh,
        in_specs=placed,
        out_specs=(
            P(("seq", "blk"), None),
            P(("seq", "blk"), None),
            P("blk", "seq", None),
            P("blk", "seq", None),
            P("blk", None, "seq"),
        ),
        check_vma=False,
    )
```

```python
import functools

import jax
import jax.numpy as jnp
from jax import lax
from jax.experimental import pallas as pl
from jax.experimental.pallas import tpu as pltpu
from jax.sharding import PartitionSpec as P

mixing_factor = 73244475
contract_last = (((1,), (1,)), ((), ()))
contract_first = (((0,), (0,)), ((), ()))
f32 = jnp.float32
bf16 = jnp.bfloat16
vmem = pl.BlockSpec(memory_space=pltpu.VMEM)
smem = pl.BlockSpec(memory_space=pltpu.SMEM)
id_lanes = 128


def scramble(values):
    values = values ^ values >> 16 & 65535
    values = values * mixing_factor
    values = values ^ values >> 16 & 65535
    values = values * mixing_factor
    return values ^ values >> 16 & 65535


def flipped(values, axis, mask):
    return lax.ppermute(values, axis, [(i, i ^ mask) for i in range(lax.axis_size(axis))])


def after(values, *earlier):
    return lax.optimization_barrier((values,) + earlier)[0]


def called(kernel, out_shape, in_specs, flops, moved, scratch=()):
    return pl.pallas_call(
        kernel,
        out_shape=out_shape,
        in_specs=in_specs,
        out_specs=jax.tree.map(lambda _: vmem, out_shape),
        scratch_shapes=list(scratch),
        compiler_params=pltpu.CompilerParams(vmem_limit_bytes=40 * 1024 * 1024),
        cost_estimate=pl.CostEstimate(flops=flops, bytes_accessed=moved, transcendentals=0),
    )


def shape(dims, kind):
    return jax.ShapeDtypeStruct(dims, kind)


def prepare_kernel(top_count, plane_experts, capacity, place_ref, table_ref, slot_ref, gate_ref):
    planes, tok_rows = table_ref.shape[1:]
    token = lax.broadcasted_iota(jnp.int32, (tok_rows, tok_rows), 0)
    later = lax.broadcasted_iota(jnp.int32, (tok_rows, tok_rows), 1)
    earlier = jnp.where(token < later, 1.0, 0.0).astype(bf16)
    place = lax.broadcasted_iota(jnp.int32, (planes, tok_rows), 0)
    for column in range(plane_experts):
        expert = place_ref[0] ^ column
        named = jnp.zeros((planes, tok_rows), f32)
        gates = jnp.zeros((planes, tok_rows), f32)
        for k in range(top_count):
            hit = table_ref[k] == expert
            named = jnp.where(hit, 1.0, named)
            gates = jnp.where(hit, table_ref[top_count + k].astype(f32), gates)
        rank = jnp.dot(named.astype(bf16), earlier, preferred_element_type=f32).astype(jnp.int32)
        slot_ref[column] = jnp.where(named > 0.0, (place >> 1) * capacity + rank, -1)
        gate_ref[column] = gates * (1.0 / 64.0)


def choice_of(slot_ref, gate_ref, column, place, rows):
    row = lax.broadcasted_iota(jnp.int32, (rows, slot_ref.shape[2]), 0)
    hit = row == slot_ref[column, place : place + 1, :]
    if gate_ref is None:
        return jnp.where(hit, 1.0, 0.0).astype(bf16)
    return jnp.where(hit, gate_ref[column, place : place + 1, :], 0.0).astype(bf16)


def compact_kernel(half, with_ids, slot_ref, gate_ref, *refs):
    plane_experts, planes, tok_rows = slot_ref.shape
    count = planes // 2
    chunk_refs, out_refs = refs[:count], refs[count:]
    stacked = jnp.concatenate([chunk[...] for chunk in chunk_refs], axis=0)
    if with_ids:
        number = lax.broadcasted_iota(jnp.int32, (tok_rows, id_lanes), 0).astype(f32).astype(bf16)
        stacked = jnp.concatenate(
            [stacked, jnp.concatenate([number] * count, axis=0)], axis=1
        )
    for column in range(plane_experts):
        choice = jnp.concatenate(
            [
                choice_of(
                    slot_ref,
                    None if with_ids else gate_ref,
                    column,
                    2 * step + half,
                    out_refs[column].shape[0],
                )
                for step in range(count)
            ],
            axis=1,
        )
        out_refs[column][...] = jnp.dot(choice, stacked, preferred_element_type=f32).astype(bf16)


def combine_kernel(half, scaled, slot_ref, gate_ref, *refs):
    plane_experts, planes, _ = slot_ref.shape
    block_refs, out_refs = refs[:plane_experts], refs[plane_experts:]
    rows = block_refs[0].shape[0]
    stacked = jnp.concatenate([block[...] for block in block_refs], axis=0)
    for step in range(planes // 2):
        choice = jnp.concatenate(
            [
                choice_of(
                    slot_ref, gate_ref if scaled else None, column, 2 * step + half, rows
                )
                for column in range(plane_experts)
            ],
            axis=0,
        )
        out_refs[step][...] = lax.dot_general(
            choice, stacked, contract_first, preferred_element_type=f32
        ).astype(out_refs[step].dtype)


def assemble(weight_ref, piece_refs, place_ref, seq_count):
    _, half_width, width = piece_refs[0].shape
    for index, piece in enumerate(piece_refs):
        part = lax.rem(place_ref[1] + index % seq_count, seq_count)
        column = pl.multiple_of(part * width, width)
        row = index // seq_count * half_width
        for kind in range(3):
            weight_ref[kind, row : row + half_width, pl.ds(column, width)] = piece[kind]


def forward_kernel(seq_count, plane_experts, planes, capacity, place_ref, key_ref, *refs):
    blocks = 2 * plane_experts
    row_refs, refs = refs[:blocks], refs[blocks:]
    piece_refs, refs = refs[: 2 * seq_count], refs[2 * seq_count :]
    out_refs, (gate_ref, up_ref, hidden_ref, weight_ref) = refs[:blocks], refs[blocks:]
    assemble(weight_ref, piece_refs, place_ref, seq_count)
    _, hidden_width, model_width = weight_ref.shape
    half_width = hidden_width // 2
    rows = row_refs[0].shape[0]
    unit = lax.broadcasted_iota(jnp.int32, (1, hidden_width), 1)
    columns = place_ref[2] + jnp.where(
        unit < half_width, unit + place_ref[3], unit - half_width + place_ref[4]
    )
    spread_columns = columns * 40503
    base_hash = scramble(key_ref[0] ^ scramble(key_ref[1]))
    inputs = jnp.concatenate([row[:, :model_width] for row in row_refs], axis=0)
    gate_pre = lax.dot_general(inputs, weight_ref[0], contract_last, preferred_element_type=f32)
    up_pre = lax.dot_general(inputs, weight_ref[1], contract_last, preferred_element_type=f32)
    shift = capacity.bit_length() - 1
    mixed = []
    for index, row in enumerate(row_refs):
        column, half = index // 2, index % 2
        within = row[:, model_width : model_width + id_lanes].astype(f32).astype(jnp.int32)
        step = lax.broadcasted_iota(jnp.int32, within.shape, 0) >> shift
        source = place_ref[5] ^ ((2 * step + half) * (2 * plane_experts) + 2 * column)
        ids = (place_ref[6] + source) * place_ref[7] + within
        mixed.append(scramble(ids ^ base_hash))
    mixed = jnp.concatenate(mixed, axis=0)[:, 0:1]
    hashed = scramble(mixed ^ spread_columns)
    keep = jnp.where((hashed & 1023) >= 128, f32(8.0 / 7.0), f32(0.0))
    sigmoid_gate = jax.nn.sigmoid(gate_pre)
    silu_gate = gate_pre * sigmoid_gate
    hidden = (silu_gate * up_pre * keep).astype(bf16)
    gate_ref[...] = up_pre * sigmoid_gate * (1.0 + gate_pre * (1.0 - sigmoid_gate)) * keep
    up_ref[...] = silu_gate * keep
    hidden_ref[...] = hidden
    expert_out = jnp.dot(hidden, weight_ref[2], preferred_element_type=f32).astype(bf16)
    for index, out in enumerate(out_refs):
        out[...] = expert_out[index * rows : (index + 1) * rows]


def backward_kernel(seq_count, plane_experts, place_ref, *refs):
    blocks = 2 * plane_experts
    cot_refs, refs = refs[:blocks], refs[blocks:]
    piece_refs, refs = refs[: 2 * seq_count], refs[2 * seq_count :]
    (gate_ref, up_ref), refs = refs[:2], refs[2:]
    out_refs, (gate_grad_ref, up_grad_ref, weight_ref) = refs[:blocks], refs[blocks:]
    assemble(weight_ref, piece_refs, place_ref, seq_count)
    rows = cot_refs[0].shape[0]
    cot = jnp.concatenate([block[...] for block in cot_refs], axis=0)
    hidden_grad = lax.dot_general(cot, weight_ref[2], contract_last, preferred_element_type=f32)
    gate_grad = (hidden_grad * gate_ref[...]).astype(bf16)
    up_grad = (hidden_grad * up_ref[...]).astype(bf16)
    gate_grad_ref[...] = gate_grad
    up_grad_ref[...] = up_grad
    input_grad = (
        jnp.dot(gate_grad, weight_ref[0], preferred_element_type=f32)
        + jnp.dot(up_grad, weight_ref[1], preferred_element_type=f32)
    ).astype(bf16)
    for index, out in enumerate(out_refs):
        out[...] = input_grad[index * rows : (index + 1) * rows]


def weight_grad_kernel(plane_experts, seq_count, shift, place_ref, *refs):
    blocks = 2 * plane_experts
    row_refs, cot_refs, refs = refs[:blocks], refs[blocks : 2 * blocks], refs[2 * blocks :]
    (hidden_ref, gate_grad_ref, up_grad_ref), refs = refs[:3], refs[3:]
    added = refs[: seq_count - 1] if shift == 0 else ()
    out_refs = refs[len(added) :]
    width = out_refs[0].shape[2]
    part = lax.rem(place_ref[1] + shift, seq_count)
    lanes = pl.ds(pl.multiple_of(part * width, width), width)
    inputs = jnp.concatenate([row[:, lanes] for row in row_refs], axis=0)
    cot = jnp.concatenate([row[:, lanes] for row in cot_refs], axis=0)
    for kind, (left, right) in enumerate(
        ((gate_grad_ref, inputs), (up_grad_ref, inputs), (hidden_ref, cot))
    ):
        total = lax.dot_general(left[...], right, contract_first, preferred_element_type=f32)
        for part_ref in added:
            total = total + part_ref[kind].astype(f32)
        if shift:
            out_refs[0][kind] = total.astype(bf16)
        else:
            half_width = total.shape[0] // 2
            out_refs[0][kind] = total[:half_width]
            out_refs[1][kind] = total[half_width:].astype(bf16)


def local(tokens, cotangent, routes, gate_codes, dropout_key, w_gate, w_up, w_down):
    seq_count = lax.axis_size("seq")
    block_count = lax.axis_size("blk")
    seq_index = lax.axis_index("seq")
    blk_index = lax.axis_index("blk")
    tok_rows, model_width = tokens.shape
    top_count = routes.shape[1]
    expert_count = block_count // 2
    capacity = 2 * tok_rows * top_count // expert_count
    half_width = w_gate.shape[2]
    part_width = w_gate.shape[1]
    hidden_width = 2 * half_width
    planes = 1 << (block_count.bit_length() // 2)
    plane_experts = expert_count // planes
    plane_stride = 2 * plane_experts
    parity = blk_index % 2
    expert_here = blk_index // 2
    rows = planes // 2 * capacity
    slot_rows = 2 * plane_experts * rows
    blocks = 2 * plane_experts
    place = jnp.stack(
        [
            expert_here,
            seq_index,
            expert_here * hidden_width,
            parity * half_width,
            (1 - parity) * half_width,
            blk_index,
            seq_index * block_count,
            jnp.int32(tok_rows),
        ]
    ).astype(jnp.int32)

    table = jnp.concatenate([routes.T, gate_codes.T], axis=0)
    tables = jnp.stack(
        [table]
        + [flipped(table, "blk", step * plane_stride) for step in range(1, planes)],
        axis=1,
    )

    own_weights = jnp.stack([w_gate[0].T, w_up[0].T, w_down[0]])
    pair_weights = flipped(own_weights, "blk", 1)

    def shifted(values, shift):
        return lax.ppermute(
            values, "seq", [(i, (i + shift) % seq_count) for i in range(seq_count)]
        )

    pieces = [
        shifted(part, -shift) if shift else part
        for part in (own_weights, pair_weights)
        for shift in range(seq_count)
    ]

    def spread(part, starts):
        chunks = {0: part}
        step = planes // 2
        while step:
            for origin in sorted(chunks):
                sent = chunks[origin]
                if origin == 0 and step in starts:
                    sent = after(sent, starts[step])
                chunks[origin ^ step] = flipped(sent, "blk", step * plane_stride)
            step //= 2
        return [chunks[origin] for origin in range(planes)]

    token_chunks = spread(tokens, {})
    cot_chunks = spread(
        cotangent, {planes // 2: token_chunks[1], 1: token_chunks[planes // 2]}
    )

    slots, gates = called(
        functools.partial(prepare_kernel, top_count, plane_experts, capacity),
        (
            shape((plane_experts, planes, tok_rows), jnp.int32),
            shape((plane_experts, planes, tok_rows), f32),
        ),
        [smem, vmem],
        10**6,
        10**5,
    )(place, tables)

    def gathered(chunks, with_ids):
        width = model_width + (id_lanes if with_ids else 0)
        found = {}
        for half in (0, 1):
            picked = chunks[half::2]
            compact = called(
                functools.partial(compact_kernel, half, with_ids),
                [shape((rows, width), bf16)] * plane_experts,
                [vmem] * (2 + len(picked)),
                2 * plane_experts * rows * len(picked) * tok_rows * width,
                4 * rows * width,
            )(slots, gates, *picked)
            for column in range(plane_experts):
                found[column, half] = (
                    flipped(compact[column], "blk", 2 * column) if column else compact[0]
                )
        return [found[column, half] for column in range(plane_experts) for half in (0, 1)]

    row_blocks = gathered(token_chunks, True)
    cot_blocks = gathered(cot_chunks, False)

    weight_scratch = pltpu.VMEM((3, hidden_width, model_width), bf16)
    flops = 2 * slot_rows * hidden_width * model_width
    *out_blocks, gate_factor, up_factor, hidden = called(
        functools.partial(forward_kernel, seq_count, plane_experts, planes, capacity),
        [shape((rows, model_width), bf16)] * blocks
        + [shape((slot_rows, hidden_width), f32)] * 2
        + [shape((slot_rows, hidden_width), bf16)],
        [smem, smem] + [vmem] * (blocks + len(pieces)),
        3 * flops,
        10**7,
        [weight_scratch],
    )(place, dropout_key, *row_blocks, *pieces)
    *grad_blocks, gate_pre_grad, up_pre_grad = called(
        functools.partial(backward_kernel, seq_count, plane_experts),
        [shape((rows, model_width), bf16)] * blocks
        + [shape((slot_rows, hidden_width), bf16)] * 2,
        [smem] + [vmem] * (blocks + len(pieces) + 2),
        3 * flops,
        10**7,
        [weight_scratch],
    )(place, *cot_blocks, *pieces, gate_factor, up_factor)

    def brought_back(slot_blocks, scaled):
        sums = {}
        for half in (1, 0):
            held = [slot_blocks[half]] + [
                flipped(slot_blocks[2 * column + half], "blk", 2 * column)
                for column in range(1, plane_experts)
            ]
            combined = called(
                functools.partial(combine_kernel, half, scaled),
                [shape((tok_rows, model_width), bf16 if half else f32)] * (planes // 2),
                [vmem] * (2 + plane_experts),
                2 * plane_experts * rows * planes // 2 * tok_rows * model_width,
                4 * rows * model_width,
            )(slots, gates, *held)
            for step in range(planes // 2):
                sums[2 * step + half] = combined[step]
        step = 1
        while step < planes:
            for origin in sorted(sums, reverse=True):
                if origin & step:
                    sums[origin ^ step] = sums[origin ^ step] + flipped(
                        sums[origin].astype(bf16), "blk", step * plane_stride
                    ).astype(f32)
                    del sums[origin]
            step *= 2
        return sums[0].astype(bf16)

    layer_out = brought_back(out_blocks, True)
    tokens_grad = brought_back(grad_blocks, False)

    def weight_grads(shift, out_shape, added):
        return called(
            functools.partial(weight_grad_kernel, plane_experts, seq_count, shift),
            out_shape,
            [smem] + [vmem] * (2 * blocks + 3 + len(added)),
            3 * flops // seq_count,
            10**7,
        )(place, *row_blocks, *cot_blocks, hidden, gate_pre_grad, up_pre_grad, *added)

    arrived = [
        shifted(
            weight_grads(shift, [shape((3, hidden_width, part_width), bf16)], [])[0], shift
        )
        for shift in range(1, seq_count)
    ]
    own_sum, pair_sum = weight_grads(
        0,
        [shape((3, half_width, part_width), f32), shape((3, half_width, part_width), bf16)],
        arrived,
    )
    grads = (own_sum + flipped(pair_sum, "blk", 1).astype(f32)).astype(bf16)
    return (layer_out, tokens_grad, grads[0].T[None], grads[1].T[None], grads[2][None])


def solution(mesh):
    placed = (
        P(("seq", "blk"), None),
        P(("seq", "blk"), None),
        P(("seq", "blk"), None),
        P(("seq", "blk"), None),
        P(),
        P("blk", "seq", None),
        P("blk", "seq", None),
        P("blk", None, "seq"),
    )
    return jax.shard_map(
        local,
        mesh=mesh,
        in_specs=placed,
        out_specs=(
            P(("seq", "blk"), None),
            P(("seq", "blk"), None),
            P("blk", "seq", None),
            P("blk", "seq", None),
            P("blk", None, "seq"),
        ),
        check_vma=False,
    )
```

```python
import functools

import jax
import jax.numpy as jnp
from jax import lax
from jax.experimental import pallas as pl
from jax.experimental.pallas import tpu as pltpu
from jax.sharding import PartitionSpec as P

mixing_factor = 73244475
contract_last = (((1,), (1,)), ((), ()))
contract_first = (((0,), (0,)), ((), ()))
f32 = jnp.float32
bf16 = jnp.bfloat16
vmem = pl.BlockSpec(memory_space=pltpu.VMEM)
smem = pl.BlockSpec(memory_space=pltpu.SMEM)
id_lanes = 128
costs = {
    "prepare": 10,
    ("inputs", 0): 20,
    ("inputs", 1): 20,
    ("cot", 0): 20,
    ("cot", 1): 20,
    "forward": 20,
    "backward": 20,
    ("out", 0): 20,
    ("out", 1): 20,
    ("grad", 0): 1,
    ("grad", 1): 1,
    "weights": 5,
}


def scramble(values):
    values = values ^ values >> 16 & 65535
    values = values * mixing_factor
    values = values ^ values >> 16 & 65535
    values = values * mixing_factor
    return values ^ values >> 16 & 65535


def flipped(values, axis, mask):
    return lax.ppermute(values, axis, [(i, i ^ mask) for i in range(lax.axis_size(axis))])


def after(values, *earlier):
    return lax.optimization_barrier((values,) + earlier)[0]


def called(kernel, out_shape, in_specs, cost, scratch=()):
    return pl.pallas_call(
        kernel,
        out_shape=out_shape,
        in_specs=in_specs,
        out_specs=jax.tree.map(lambda _: vmem, out_shape),
        scratch_shapes=list(scratch),
        compiler_params=pltpu.CompilerParams(vmem_limit_bytes=40 * 1024 * 1024),
        cost_estimate=pl.CostEstimate(
            flops=cost * 10**9, bytes_accessed=cost * 3 * 10**6, transcendentals=0
        ),
    )


def shape(dims, kind):
    return jax.ShapeDtypeStruct(dims, kind)


def prepare_kernel(top_count, plane_experts, capacity, place_ref, table_ref, slot_ref, gate_ref):
    planes, tok_rows = table_ref.shape[1:]
    token = lax.broadcasted_iota(jnp.int32, (tok_rows, tok_rows), 0)
    later = lax.broadcasted_iota(jnp.int32, (tok_rows, tok_rows), 1)
    earlier = jnp.where(token < later, 1.0, 0.0).astype(bf16)
    place = lax.broadcasted_iota(jnp.int32, (planes, tok_rows), 0)
    for column in range(plane_experts):
        expert = place_ref[0] ^ column
        named = jnp.zeros((planes, tok_rows), f32)
        gates = jnp.zeros((planes, tok_rows), f32)
        for k in range(top_count):
            hit = table_ref[k] == expert
            named = jnp.where(hit, 1.0, named)
            gates = jnp.where(hit, table_ref[top_count + k].astype(f32), gates)
        rank = jnp.dot(named.astype(bf16), earlier, preferred_element_type=f32).astype(jnp.int32)
        slot_ref[column] = jnp.where(named > 0.0, (place >> 1) * capacity + rank, -1)
        gate_ref[column] = gates * (1.0 / 64.0)


def choice_of(slot_ref, gate_ref, column, place, rows):
    row = lax.broadcasted_iota(jnp.int32, (rows, slot_ref.shape[2]), 0)
    hit = row == slot_ref[column, place : place + 1, :]
    if gate_ref is None:
        return jnp.where(hit, 1.0, 0.0).astype(bf16)
    return jnp.where(hit, gate_ref[column, place : place + 1, :], 0.0).astype(bf16)


def compact_kernel(half, with_ids, slot_ref, gate_ref, *refs):
    plane_experts, planes, tok_rows = slot_ref.shape
    count = planes // 2
    chunk_refs, out_refs = refs[:count], refs[count:]
    stacked = jnp.concatenate([chunk[...] for chunk in chunk_refs], axis=0)
    if with_ids:
        number = lax.broadcasted_iota(jnp.int32, (tok_rows, id_lanes), 0).astype(f32).astype(bf16)
        stacked = jnp.concatenate(
            [stacked, jnp.concatenate([number] * count, axis=0)], axis=1
        )
    for column in range(plane_experts):
        choice = jnp.concatenate(
            [
                choice_of(
                    slot_ref,
                    None if with_ids else gate_ref,
                    column,
                    2 * step + half,
                    out_refs[column].shape[0],
                )
                for step in range(count)
            ],
            axis=1,
        )
        out_refs[column][...] = jnp.dot(choice, stacked, preferred_element_type=f32).astype(bf16)


def combine_kernel(half, scaled, slot_ref, gate_ref, *refs):
    plane_experts, planes, _ = slot_ref.shape
    block_refs, out_refs = refs[:plane_experts], refs[plane_experts:]
    rows = block_refs[0].shape[0]
    stacked = jnp.concatenate([block[...] for block in block_refs], axis=0)
    for step in range(planes // 2):
        choice = jnp.concatenate(
            [
                choice_of(
                    slot_ref, gate_ref if scaled else None, column, 2 * step + half, rows
                )
                for column in range(plane_experts)
            ],
            axis=0,
        )
        out_refs[step][...] = lax.dot_general(
            choice, stacked, contract_first, preferred_element_type=f32
        ).astype(out_refs[step].dtype)


def assemble(weight_ref, piece_refs, place_ref, seq_count):
    _, half_width, width = piece_refs[0].shape
    for index, piece in enumerate(piece_refs):
        part = lax.rem(place_ref[1] + index % seq_count, seq_count)
        column = pl.multiple_of(part * width, width)
        row = index // seq_count * half_width
        for kind in range(3):
            weight_ref[kind, row : row + half_width, pl.ds(column, width)] = piece[kind]


def forward_kernel(seq_count, plane_experts, planes, capacity, place_ref, key_ref, *refs):
    blocks = 2 * plane_experts
    row_refs, refs = refs[:blocks], refs[blocks:]
    piece_refs, refs = refs[: 2 * seq_count], refs[2 * seq_count :]
    out_refs, (gate_ref, up_ref, hidden_ref, weight_ref) = refs[:blocks], refs[blocks:]
    assemble(weight_ref, piece_refs, place_ref, seq_count)
    _, hidden_width, model_width = weight_ref.shape
    half_width = hidden_width // 2
    rows = row_refs[0].shape[0]
    unit = lax.broadcasted_iota(jnp.int32, (1, hidden_width), 1)
    columns = place_ref[2] + jnp.where(
        unit < half_width, unit + place_ref[3], unit - half_width + place_ref[4]
    )
    spread_columns = columns * 40503
    base_hash = scramble(key_ref[0] ^ scramble(key_ref[1]))
    inputs = jnp.concatenate([row[:, :model_width] for row in row_refs], axis=0)
    gate_pre = lax.dot_general(inputs, weight_ref[0], contract_last, preferred_element_type=f32)
    up_pre = lax.dot_general(inputs, weight_ref[1], contract_last, preferred_element_type=f32)
    shift = capacity.bit_length() - 1
    mixed = []
    for index, row in enumerate(row_refs):
        column, half = index // 2, index % 2
        within = row[:, model_width : model_width + id_lanes].astype(f32).astype(jnp.int32)
        step = lax.broadcasted_iota(jnp.int32, within.shape, 0) >> shift
        source = place_ref[5] ^ ((2 * step + half) * (2 * plane_experts) + 2 * column)
        ids = (place_ref[6] + source) * place_ref[7] + within
        mixed.append(scramble(ids ^ base_hash))
    mixed = jnp.concatenate(mixed, axis=0)[:, 0:1]
    hashed = scramble(mixed ^ spread_columns)
    keep = jnp.where((hashed & 1023) >= 128, f32(8.0 / 7.0), f32(0.0))
    sigmoid_gate = jax.nn.sigmoid(gate_pre)
    silu_gate = gate_pre * sigmoid_gate
    hidden = (silu_gate * up_pre * keep).astype(bf16)
    gate_ref[...] = up_pre * sigmoid_gate * (1.0 + gate_pre * (1.0 - sigmoid_gate)) * keep
    up_ref[...] = silu_gate * keep
    hidden_ref[...] = hidden
    expert_out = jnp.dot(hidden, weight_ref[2], preferred_element_type=f32).astype(bf16)
    for index, out in enumerate(out_refs):
        out[...] = expert_out[index * rows : (index + 1) * rows]


def backward_kernel(seq_count, plane_experts, place_ref, *refs):
    blocks = 2 * plane_experts
    cot_refs, refs = refs[:blocks], refs[blocks:]
    piece_refs, refs = refs[: 2 * seq_count], refs[2 * seq_count :]
    (gate_ref, up_ref), refs = refs[:2], refs[2:]
    out_refs, (gate_grad_ref, up_grad_ref, weight_ref) = refs[:blocks], refs[blocks:]
    assemble(weight_ref, piece_refs, place_ref, seq_count)
    rows = cot_refs[0].shape[0]
    cot = jnp.concatenate([block[...] for block in cot_refs], axis=0)
    hidden_grad = lax.dot_general(cot, weight_ref[2], contract_last, preferred_element_type=f32)
    gate_grad = (hidden_grad * gate_ref[...]).astype(bf16)
    up_grad = (hidden_grad * up_ref[...]).astype(bf16)
    gate_grad_ref[...] = gate_grad
    up_grad_ref[...] = up_grad
    input_grad = (
        jnp.dot(gate_grad, weight_ref[0], preferred_element_type=f32)
        + jnp.dot(up_grad, weight_ref[1], preferred_element_type=f32)
    ).astype(bf16)
    for index, out in enumerate(out_refs):
        out[...] = input_grad[index * rows : (index + 1) * rows]


def weight_grad_kernel(plane_experts, seq_count, shift, place_ref, *refs):
    blocks = 2 * plane_experts
    row_refs, cot_refs, refs = refs[:blocks], refs[blocks : 2 * blocks], refs[2 * blocks :]
    (hidden_ref, gate_grad_ref, up_grad_ref), refs = refs[:3], refs[3:]
    added = refs[: seq_count - 1] if shift == 0 else ()
    out_refs = refs[len(added) :]
    width = out_refs[0].shape[2]
    part = lax.rem(place_ref[1] + shift, seq_count)
    lanes = pl.ds(pl.multiple_of(part * width, width), width)
    inputs = jnp.concatenate([row[:, lanes] for row in row_refs], axis=0)
    cot = jnp.concatenate([row[:, lanes] for row in cot_refs], axis=0)
    for kind, (left, right) in enumerate(
        ((gate_grad_ref, inputs), (up_grad_ref, inputs), (hidden_ref, cot))
    ):
        total = lax.dot_general(left[...], right, contract_first, preferred_element_type=f32)
        for part_ref in added:
            total = total + part_ref[kind].astype(f32)
        if shift:
            out_refs[0][kind] = total.astype(bf16)
        else:
            half_width = total.shape[0] // 2
            out_refs[0][kind] = total[:half_width]
            out_refs[1][kind] = total[half_width:].astype(bf16)


def local(tokens, cotangent, routes, gate_codes, dropout_key, w_gate, w_up, w_down):
    seq_count = lax.axis_size("seq")
    block_count = lax.axis_size("blk")
    seq_index = lax.axis_index("seq")
    blk_index = lax.axis_index("blk")
    tok_rows, model_width = tokens.shape
    top_count = routes.shape[1]
    expert_count = block_count // 2
    capacity = 2 * tok_rows * top_count // expert_count
    half_width = w_gate.shape[2]
    part_width = w_gate.shape[1]
    hidden_width = 2 * half_width
    planes = 1 << (block_count.bit_length() // 2)
    plane_experts = expert_count // planes
    plane_stride = 2 * plane_experts
    parity = blk_index % 2
    expert_here = blk_index // 2
    rows = planes // 2 * capacity
    slot_rows = 2 * plane_experts * rows
    blocks = 2 * plane_experts
    place = jnp.stack(
        [
            expert_here,
            seq_index,
            expert_here * hidden_width,
            parity * half_width,
            (1 - parity) * half_width,
            blk_index,
            seq_index * block_count,
            jnp.int32(tok_rows),
        ]
    ).astype(jnp.int32)

    table = jnp.concatenate([routes.T, gate_codes.T], axis=0)
    tables = jnp.stack(
        [table]
        + [flipped(table, "blk", step * plane_stride) for step in range(1, planes)],
        axis=1,
    )

    own_weights = jnp.stack([w_gate[0].T, w_up[0].T, w_down[0]])
    pair_weights = flipped(own_weights, "blk", 1)

    def shifted(values, shift):
        return lax.ppermute(
            values, "seq", [(i, (i + shift) % seq_count) for i in range(seq_count)]
        )

    pieces = [
        shifted(part, -shift) if shift else part
        for part in (own_weights, pair_weights)
        for shift in range(seq_count)
    ]

    def spread(part, starts):
        chunks = {0: part}
        step = planes // 2
        while step:
            for origin in sorted(chunks):
                sent = chunks[origin]
                if origin == 0 and step in starts:
                    sent = after(sent, starts[step])
                chunks[origin ^ step] = flipped(sent, "blk", step * plane_stride)
            step //= 2
        return [chunks[origin] for origin in range(planes)]

    token_chunks = spread(tokens, {})
    cot_chunks = spread(
        cotangent, {planes // 2: token_chunks[1], 1: token_chunks[planes // 2]}
    )

    slots, gates = called(
        functools.partial(prepare_kernel, top_count, plane_experts, capacity),
        (
            shape((plane_experts, planes, tok_rows), jnp.int32),
            shape((plane_experts, planes, tok_rows), f32),
        ),
        [smem, vmem],
        costs["prepare"],
    )(place, tables)

    def gathered(chunks, with_ids):
        width = model_width + (id_lanes if with_ids else 0)
        found = {}
        for half in (0, 1):
            picked = chunks[half::2]
            compact = called(
                functools.partial(compact_kernel, half, with_ids),
                [shape((rows, width), bf16)] * plane_experts,
                [vmem] * (2 + len(picked)),
                costs["inputs" if with_ids else "cot", half],
            )(slots, gates, *picked)
            for column in range(plane_experts):
                found[column, half] = (
                    flipped(compact[column], "blk", 2 * column) if column else compact[0]
                )
        return [found[column, half] for column in range(plane_experts) for half in (0, 1)]

    row_blocks = gathered(token_chunks, True)
    cot_blocks = gathered(cot_chunks, False)

    weight_scratch = pltpu.VMEM((3, hidden_width, model_width), bf16)
    *out_blocks, gate_factor, up_factor, hidden = called(
        functools.partial(forward_kernel, seq_count, plane_experts, planes, capacity),
        [shape((rows, model_width), bf16)] * blocks
        + [shape((slot_rows, hidden_width), f32)] * 2
        + [shape((slot_rows, hidden_width), bf16)],
        [smem, smem] + [vmem] * (blocks + len(pieces)),
        costs["forward"],
        [weight_scratch],
    )(place, dropout_key, *row_blocks, *pieces)
    *grad_blocks, gate_pre_grad, up_pre_grad = called(
        functools.partial(backward_kernel, seq_count, plane_experts),
        [shape((rows, model_width), bf16)] * blocks
        + [shape((slot_rows, hidden_width), bf16)] * 2,
        [smem] + [vmem] * (blocks + len(pieces) + 2),
        costs["backward"],
        [weight_scratch],
    )(place, *cot_blocks, *pieces, gate_factor, up_factor)

    def brought_back(slot_blocks, scaled):
        sums = {}
        for half in (1, 0):
            held = [slot_blocks[half]] + [
                flipped(slot_blocks[2 * column + half], "blk", 2 * column)
                for column in range(1, plane_experts)
            ]
            combined = called(
                functools.partial(combine_kernel, half, scaled),
                [shape((tok_rows, model_width), bf16 if half else f32)] * (planes // 2),
                [vmem] * (2 + plane_experts),
                costs["out" if scaled else "grad", half],
            )(slots, gates, *held)
            for step in range(planes // 2):
                sums[2 * step + half] = combined[step]
        step = 1
        while step < planes:
            for origin in sorted(sums, reverse=True):
                if origin & step:
                    sums[origin ^ step] = sums[origin ^ step] + flipped(
                        sums[origin].astype(bf16), "blk", step * plane_stride
                    ).astype(f32)
                    del sums[origin]
            step *= 2
        return sums[0].astype(bf16)

    layer_out = brought_back(out_blocks, True)
    tokens_grad = brought_back(grad_blocks, False)

    def weight_grads(shift, out_shape, added):
        return called(
            functools.partial(weight_grad_kernel, plane_experts, seq_count, shift),
            out_shape,
            [smem] + [vmem] * (2 * blocks + 3 + len(added)),
            costs["weights"],
        )(place, *row_blocks, *cot_blocks, hidden, gate_pre_grad, up_pre_grad, *added)

    arrived = [
        shifted(
            weight_grads(shift, [shape((3, hidden_width, part_width), bf16)], [])[0], shift
        )
        for shift in range(1, seq_count)
    ]
    own_sum, pair_sum = weight_grads(
        0,
        [shape((3, half_width, part_width), f32), shape((3, half_width, part_width), bf16)],
        arrived,
    )
    grads = (own_sum + flipped(pair_sum, "blk", 1).astype(f32)).astype(bf16)
    return (layer_out, tokens_grad, grads[0].T[None], grads[1].T[None], grads[2][None])


def solution(mesh):
    placed = (
        P(("seq", "blk"), None),
        P(("seq", "blk"), None),
        P(("seq", "blk"), None),
        P(("seq", "blk"), None),
        P(),
        P("blk", "seq", None),
        P("blk", "seq", None),
        P("blk", None, "seq"),
    )
    return jax.shard_map(
        local,
        mesh=mesh,
        in_specs=placed,
        out_specs=(
            P(("seq", "blk"), None),
            P(("seq", "blk"), None),
            P("blk", "seq", None),
            P("blk", "seq", None),
            P("blk", None, "seq"),
        ),
        check_vma=False,
    )
```

```python
import functools

import jax
import jax.numpy as jnp
from jax import lax
from jax.experimental import pallas as pl
from jax.experimental.pallas import tpu as pltpu
from jax.sharding import PartitionSpec as P

mixing_factor = 73244475
contract_last = (((1,), (1,)), ((), ()))
contract_first = (((0,), (0,)), ((), ()))
f32 = jnp.float32
bf16 = jnp.bfloat16
vmem = pl.BlockSpec(memory_space=pltpu.VMEM)
smem = pl.BlockSpec(memory_space=pltpu.SMEM)
id_lanes = 128
costs = {
    "prep": 10,
    "pt0": 20,
    "pt1": 20,
    "pc0": 20,
    "pc1": 20,
    "fwd": 20,
    "bwd": 20,
    "co0": 20,
    "co1": 20,
    "cg0": 1,
    "cg1": 1,
    "ddk1": 5,
    "ddk0": 5,
    "dik1": 5,
    "dik0": 5,
}
order = {
    "t3": ("t1",),
    "c2": ("t1", "t2",),
    "c3": ("t3", "yt0", "wx",),
    "c1": ("t3", "c2", "yt0",),
    "pc0": ("yt0", "pt1",),
    "wp1": ("c2", "t3",),
    "pc1": ("yt1", "yc0", "wp1",),
    "bwd": ("yo1",),
    "o": ("cg0",),
    "ws1": ("T2",),
}


def scramble(values):
    values = values ^ values >> 16 & 65535
    values = values * mixing_factor
    values = values ^ values >> 16 & 65535
    values = values * mixing_factor
    return values ^ values >> 16 & 65535


def flipped(values, axis, mask):
    return lax.ppermute(values, axis, [(i, i ^ mask) for i in range(lax.axis_size(axis))])


def after(values, *earlier):
    return lax.optimization_barrier((values,) + earlier)[0]


def called(kernel, out_shape, in_specs, cost, scratch=()):
    return pl.pallas_call(
        kernel,
        out_shape=out_shape,
        in_specs=in_specs,
        out_specs=jax.tree.map(lambda _: vmem, out_shape),
        scratch_shapes=list(scratch),
        compiler_params=pltpu.CompilerParams(vmem_limit_bytes=40 * 1024 * 1024),
        cost_estimate=pl.CostEstimate(
            flops=cost * 10**9, bytes_accessed=cost * 3 * 10**6, transcendentals=0
        ),
    )


def shape(dims, kind):
    return jax.ShapeDtypeStruct(dims, kind)


def prepare_kernel(top_count, plane_experts, capacity, place_ref, table_ref, slot_ref, gate_ref):
    planes, tok_rows = table_ref.shape[1:]
    token = lax.broadcasted_iota(jnp.int32, (tok_rows, tok_rows), 0)
    later = lax.broadcasted_iota(jnp.int32, (tok_rows, tok_rows), 1)
    earlier = jnp.where(token < later, 1.0, 0.0).astype(bf16)
    place = lax.broadcasted_iota(jnp.int32, (planes, tok_rows), 0)
    for column in range(plane_experts):
        expert = place_ref[0] ^ column
        named = jnp.zeros((planes, tok_rows), f32)
        gates = jnp.zeros((planes, tok_rows), f32)
        for k in range(top_count):
            hit = table_ref[k] == expert
            named = jnp.where(hit, 1.0, named)
            gates = jnp.where(hit, table_ref[top_count + k].astype(f32), gates)
        rank = jnp.dot(named.astype(bf16), earlier, preferred_element_type=f32).astype(jnp.int32)
        slot_ref[column] = jnp.where(named > 0.0, (place >> 1) * capacity + rank, -1)
        gate_ref[column] = gates * (1.0 / 64.0)


def choice_of(slot_ref, gate_ref, column, place, rows):
    row = lax.broadcasted_iota(jnp.int32, (rows, slot_ref.shape[2]), 0)
    hit = row == slot_ref[column, place : place + 1, :]
    if gate_ref is None:
        return jnp.where(hit, 1.0, 0.0).astype(bf16)
    return jnp.where(hit, gate_ref[column, place : place + 1, :], 0.0).astype(bf16)


def compact_kernel(half, with_ids, slot_ref, gate_ref, *refs):
    plane_experts, planes, tok_rows = slot_ref.shape
    count = planes // 2
    chunk_refs, out_refs = refs[:count], refs[count:]
    stacked = jnp.concatenate([chunk[...] for chunk in chunk_refs], axis=0)
    if with_ids:
        number = lax.broadcasted_iota(jnp.int32, (tok_rows, id_lanes), 0).astype(f32).astype(bf16)
        stacked = jnp.concatenate(
            [stacked, jnp.concatenate([number] * count, axis=0)], axis=1
        )
    for column in range(plane_experts):
        choice = jnp.concatenate(
            [
                choice_of(
                    slot_ref,
                    None if with_ids else gate_ref,
                    column,
                    2 * step + half,
                    out_refs[column].shape[0],
                )
                for step in range(count)
            ],
            axis=1,
        )
        out_refs[column][...] = jnp.dot(choice, stacked, preferred_element_type=f32).astype(bf16)


def combine_kernel(half, scaled, slot_ref, gate_ref, *refs):
    plane_experts, planes, _ = slot_ref.shape
    block_refs, out_refs = refs[:plane_experts], refs[plane_experts:]
    rows = block_refs[0].shape[0]
    stacked = jnp.concatenate([block[...] for block in block_refs], axis=0)
    for step in range(planes // 2):
        choice = jnp.concatenate(
            [
                choice_of(
                    slot_ref, gate_ref if scaled else None, column, 2 * step + half, rows
                )
                for column in range(plane_experts)
            ],
            axis=0,
        )
        out_refs[step][...] = lax.dot_general(
            choice, stacked, contract_first, preferred_element_type=f32
        ).astype(out_refs[step].dtype)


def assemble(weight_ref, piece_refs, place_ref, seq_count):
    _, half_width, width = piece_refs[0].shape
    for index, piece in enumerate(piece_refs):
        part = lax.rem(place_ref[1] + index % seq_count, seq_count)
        column = pl.multiple_of(part * width, width)
        row = index // seq_count * half_width
        for kind in range(3):
            weight_ref[kind, row : row + half_width, pl.ds(column, width)] = piece[kind]


def forward_kernel(seq_count, plane_experts, planes, capacity, place_ref, key_ref, *refs):
    blocks = 2 * plane_experts
    row_refs, refs = refs[:blocks], refs[blocks:]
    piece_refs, refs = refs[: 2 * seq_count], refs[2 * seq_count :]
    out_refs, (gate_ref, up_ref, hidden_ref, weight_ref) = refs[:blocks], refs[blocks:]
    assemble(weight_ref, piece_refs, place_ref, seq_count)
    _, hidden_width, model_width = weight_ref.shape
    half_width = hidden_width // 2
    rows = row_refs[0].shape[0]
    unit = lax.broadcasted_iota(jnp.int32, (1, hidden_width), 1)
    columns = place_ref[2] + jnp.where(
        unit < half_width, unit + place_ref[3], unit - half_width + place_ref[4]
    )
    spread_columns = columns * 40503
    base_hash = scramble(key_ref[0] ^ scramble(key_ref[1]))
    inputs = jnp.concatenate([row[:, :model_width] for row in row_refs], axis=0)
    gate_pre = lax.dot_general(inputs, weight_ref[0], contract_last, preferred_element_type=f32)
    up_pre = lax.dot_general(inputs, weight_ref[1], contract_last, preferred_element_type=f32)
    shift = capacity.bit_length() - 1
    mixed = []
    for index, row in enumerate(row_refs):
        column, half = index // 2, index % 2
        within = row[:, model_width : model_width + id_lanes].astype(f32).astype(jnp.int32)
        step = lax.broadcasted_iota(jnp.int32, within.shape, 0) >> shift
        source = place_ref[5] ^ ((2 * step + half) * (2 * plane_experts) + 2 * column)
        ids = (place_ref[6] + source) * place_ref[7] + within
        mixed.append(scramble(ids ^ base_hash))
    mixed = jnp.concatenate(mixed, axis=0)[:, 0:1]
    hashed = scramble(mixed ^ spread_columns)
    keep = jnp.where((hashed & 1023) >= 128, f32(8.0 / 7.0), f32(0.0))
    sigmoid_gate = jax.nn.sigmoid(gate_pre)
    silu_gate = gate_pre * sigmoid_gate
    hidden = (silu_gate * up_pre * keep).astype(bf16)
    gate_ref[...] = up_pre * sigmoid_gate * (1.0 + gate_pre * (1.0 - sigmoid_gate)) * keep
    up_ref[...] = silu_gate * keep
    hidden_ref[...] = hidden
    expert_out = jnp.dot(hidden, weight_ref[2], preferred_element_type=f32).astype(bf16)
    for index, out in enumerate(out_refs):
        out[...] = expert_out[index * rows : (index + 1) * rows]


def backward_kernel(seq_count, plane_experts, place_ref, *refs):
    blocks = 2 * plane_experts
    cot_refs, refs = refs[:blocks], refs[blocks:]
    piece_refs, refs = refs[: 2 * seq_count], refs[2 * seq_count :]
    (gate_ref, up_ref), refs = refs[:2], refs[2:]
    out_refs, (gate_grad_ref, up_grad_ref, weight_ref) = refs[:blocks], refs[blocks:]
    assemble(weight_ref, piece_refs, place_ref, seq_count)
    rows = cot_refs[0].shape[0]
    cot = jnp.concatenate([block[...] for block in cot_refs], axis=0)
    hidden_grad = lax.dot_general(cot, weight_ref[2], contract_last, preferred_element_type=f32)
    gate_grad = (hidden_grad * gate_ref[...]).astype(bf16)
    up_grad = (hidden_grad * up_ref[...]).astype(bf16)
    gate_grad_ref[...] = gate_grad
    up_grad_ref[...] = up_grad
    input_grad = (
        jnp.dot(gate_grad, weight_ref[0], preferred_element_type=f32)
        + jnp.dot(up_grad, weight_ref[1], preferred_element_type=f32)
    ).astype(bf16)
    for index, out in enumerate(out_refs):
        out[...] = input_grad[index * rows : (index + 1) * rows]


def weight_grad_kernel(blocks, seq_count, shift, kinds, place_ref, *refs):
    row_refs, refs = refs[:blocks], refs[blocks:]
    left_refs, refs = refs[:kinds], refs[kinds:]
    added = refs[: seq_count - 1] if shift == 0 else ()
    out_refs = refs[len(added) :]
    width = out_refs[0].shape[2]
    part = lax.rem(place_ref[1] + shift, seq_count)
    lanes = pl.ds(pl.multiple_of(part * width, width), width)
    right = jnp.concatenate([row[:, lanes] for row in row_refs], axis=0)
    for kind, left in enumerate(left_refs):
        total = lax.dot_general(left[...], right, contract_first, preferred_element_type=f32)
        for part_ref in added:
            total = total + part_ref[kind].astype(f32)
        if shift:
            out_refs[0][kind] = total.astype(bf16)
        else:
            half_width = total.shape[0] // 2
            out_refs[0][kind] = total[:half_width]
            out_refs[1][kind] = total[half_width:].astype(bf16)


def local(tokens, cotangent, routes, gate_codes, dropout_key, w_gate, w_up, w_down):
    seq_count = lax.axis_size("seq")
    block_count = lax.axis_size("blk")
    seq_index = lax.axis_index("seq")
    blk_index = lax.axis_index("blk")
    tok_rows, model_width = tokens.shape
    top_count = routes.shape[1]
    expert_count = block_count // 2
    capacity = 2 * tok_rows * top_count // expert_count
    half_width = w_gate.shape[2]
    part_width = w_gate.shape[1]
    hidden_width = 2 * half_width
    planes = 1 << (block_count.bit_length() // 2)
    plane_experts = expert_count // planes
    plane_stride = 2 * plane_experts
    parity = blk_index % 2
    expert_here = blk_index // 2
    rows = planes // 2 * capacity
    slot_rows = 2 * plane_experts * rows
    blocks = 2 * plane_experts
    place = jnp.stack(
        [
            expert_here,
            seq_index,
            expert_here * hidden_width,
            parity * half_width,
            (1 - parity) * half_width,
            blk_index,
            seq_index * block_count,
            jnp.int32(tok_rows),
        ]
    ).astype(jnp.int32)

    steps = {}
    made = {}

    def step(name, build):
        steps[name] = build

    def get(name):
        if name not in made:
            waits = [jax.tree.leaves(get(other))[-1] for other in order.get(name, ())]
            made[name] = steps[name](lambda value: after(value, *waits) if waits else value)
        return made[name]

    def across(mask):
        return lambda value: flipped(value, "blk", mask)

    def low_bit(origin):
        return origin & -origin

    def shifted(values, shift):
        return lax.ppermute(
            values, "seq", [(i, (i + shift) % seq_count) for i in range(seq_count)]
        )

    table = jnp.concatenate([routes.T, gate_codes.T], axis=0)
    for origin in range(1, planes):
        step(
            f"T{origin}",
            lambda wait, origin=origin: flipped(wait(table), "blk", origin * plane_stride),
        )

    for kind, part in (("t", tokens), ("c", cotangent)):
        step(f"{kind}0", lambda wait, part=part: part)
        for origin in range(1, planes):
            step(
                f"{kind}{origin}",
                lambda wait, kind=kind, origin=origin: flipped(
                    wait(get(f"{kind}{origin - low_bit(origin)}")),
                    "blk",
                    low_bit(origin) * plane_stride,
                ),
            )

    own_weights = jnp.stack([w_gate[0].T, w_up[0].T, w_down[0]])
    step("wx", lambda wait: flipped(wait(own_weights), "blk", 1))
    for shift in range(1, seq_count):
        step(f"ws{shift}", lambda wait, shift=shift: shifted(wait(own_weights), -shift))
        step(f"wp{shift}", lambda wait, shift=shift: shifted(wait(get("wx")), -shift))

    def pieces():
        others = range(1, seq_count)
        return [own_weights, *(get(f"ws{k}") for k in others)] + [
            get("wx"),
            *(get(f"wp{k}") for k in others),
        ]

    step(
        "prep",
        lambda wait: called(
            functools.partial(prepare_kernel, top_count, plane_experts, capacity),
            (
                shape((plane_experts, planes, tok_rows), jnp.int32),
                shape((plane_experts, planes, tok_rows), f32),
            ),
            [smem, vmem],
            costs["prep"],
        )(
            place,
            wait(jnp.stack([table] + [get(f"T{k}") for k in range(1, planes)], axis=1)),
        ),
    )

    def packed(kind, half, wait):
        width = model_width + (id_lanes if kind == "t" else 0)
        chunks = [get(f"{kind}{origin}") for origin in range(half, planes, 2)]
        chunks[0] = wait(chunks[0])
        return called(
            functools.partial(compact_kernel, half, kind == "t"),
            [shape((rows, width), bf16)] * plane_experts,
            [vmem] * (2 + len(chunks)),
            costs[f"p{kind}{half}"],
        )(*get("prep"), *chunks)

    def exchanged(blocks_out, wait):
        return [
            flipped(wait(blocks_out[column]), "blk", 2 * column)
            for column in range(1, plane_experts)
        ]

    for kind in "tc":
        for half in (0, 1):
            step(f"p{kind}{half}", lambda wait, kind=kind, half=half: packed(kind, half, wait))
            step(
                f"y{kind}{half}",
                lambda wait, kind=kind, half=half: exchanged(get(f"p{kind}{half}"), wait),
            )

    def row_blocks(kind):
        halves = [[get(f"p{kind}{half}")[0], *get(f"y{kind}{half}")] for half in (0, 1)]
        return [block for pair in zip(*halves) for block in pair]

    weight_scratch = pltpu.VMEM((3, hidden_width, model_width), bf16)

    def forward(wait):
        row_parts, piece_parts = row_blocks("t"), pieces()
        row_parts[0] = wait(row_parts[0])
        return called(
            functools.partial(forward_kernel, seq_count, plane_experts, planes, capacity),
            [shape((rows, model_width), bf16)] * blocks
            + [shape((slot_rows, hidden_width), f32)] * 2
            + [shape((slot_rows, hidden_width), bf16)],
            [smem, smem] + [vmem] * (blocks + len(piece_parts)),
            costs["fwd"],
            [weight_scratch],
        )(place, dropout_key, *row_parts, *piece_parts)

    def backward(wait):
        cot_parts, piece_parts = row_blocks("c"), pieces()
        cot_parts[0] = wait(cot_parts[0])
        return called(
            functools.partial(backward_kernel, seq_count, plane_experts),
            [shape((rows, model_width), bf16)] * blocks
            + [shape((slot_rows, hidden_width), bf16)] * 2,
            [smem] + [vmem] * (blocks + len(piece_parts) + 2),
            costs["bwd"],
            [weight_scratch],
        )(place, *cot_parts, *piece_parts, *get("fwd")[blocks : blocks + 2])

    step("fwd", forward)
    step("bwd", backward)

    def combined(kind, half, wait):
        source = get("fwd" if kind == "o" else "bwd")
        held = [wait(source[half]), *get(f"y{kind}{half}")]
        return called(
            functools.partial(combine_kernel, half, kind == "o"),
            [shape((tok_rows, model_width), bf16 if half else f32)] * (planes // 2),
            [vmem] * (2 + plane_experts),
            costs[f"c{kind}{half}"],
        )(*get("prep"), *held)

    def total(kind, origin):
        value = get(f"c{kind}{origin % 2}")[origin // 2]
        for other in range(origin + 1, planes):
            if other - low_bit(other) == origin:
                value = value.astype(f32) + get(f"z{kind}{other}").astype(f32)
        return value.astype(bf16)

    for kind in "og":
        for half in (0, 1):
            step(
                f"y{kind}{half}",
                lambda wait, kind=kind, half=half: exchanged(
                    [
                        get("fwd" if kind == "o" else "bwd")[2 * column + half]
                        for column in range(plane_experts)
                    ],
                    wait,
                ),
            )
            step(f"c{kind}{half}", lambda wait, kind=kind, half=half: combined(kind, half, wait))
        for origin in range(1, planes):
            step(
                f"z{kind}{origin}",
                lambda wait, kind=kind, origin=origin: flipped(
                    wait(total(kind, origin)), "blk", low_bit(origin) * plane_stride
                ),
            )
        step(f"{kind}", lambda wait, kind=kind: wait(total(kind, 0)))

    def weight_kernel(name, wait, shift):
        if name == "dd":
            row_parts, lefts = row_blocks("c"), [get("fwd")[blocks + 2]]
        else:
            row_parts, lefts = row_blocks("t"), get("bwd")[blocks:]
        kinds = len(lefts)
        arrived = [] if shift else [get(f"{name}s{k}") for k in range(1, seq_count)]
        lefts = [wait(lefts[0]), *lefts[1:]]
        if shift:
            result = [shape((kinds, hidden_width, part_width), bf16)]
        else:
            result = [
                shape((kinds, half_width, part_width), f32),
                shape((kinds, half_width, part_width), bf16),
            ]
        return called(
            functools.partial(weight_grad_kernel, blocks, seq_count, shift, kinds),
            result,
            [smem] + [vmem] * (blocks + kinds + len(arrived)),
            costs[f"{name}k{min(shift, 1)}"],
        )(place, *row_parts, *lefts, *arrived)

    for name in ("dd", "di"):
        for shift in range(seq_count):
            step(
                f"{name}k{shift}",
                lambda wait, name=name, shift=shift: weight_kernel(name, wait, shift),
            )
            step(
                f"{name}s{shift}",
                lambda wait, name=name, shift=shift: shifted(
                    wait(get(f"{name}k{shift}")[0]), shift
                ),
            )
        step(f"{name}x", lambda wait, name=name: across(1)(wait(get(f"{name}k0")[1])))
        step(
            name,
            lambda wait, name=name: (
                wait(get(f"{name}k0")[0]) + get(f"{name}x").astype(f32)
            ).astype(bf16),
        )

    down_grad, input_grads = get("dd"), get("di")
    return (
        get("o"),
        get("g"),
        input_grads[0].T[None],
        input_grads[1].T[None],
        down_grad,
    )


def solution(mesh):
    placed = (
        P(("seq", "blk"), None),
        P(("seq", "blk"), None),
        P(("seq", "blk"), None),
        P(("seq", "blk"), None),
        P(),
        P("blk", "seq", None),
        P("blk", "seq", None),
        P("blk", None, "seq"),
    )
    return jax.shard_map(
        local,
        mesh=mesh,
        in_specs=placed,
        out_specs=(
            P(("seq", "blk"), None),
            P(("seq", "blk"), None),
            P("blk", "seq", None),
            P("blk", "seq", None),
            P("blk", None, "seq"),
        ),
        check_vma=False,
    )
```

```python
import functools

import jax
import jax.numpy as jnp
from jax import lax
from jax.experimental import pallas as pl
from jax.experimental.pallas import tpu as pltpu
from jax.sharding import PartitionSpec as P

mixing_factor = 73244475
contract_last = (((1,), (1,)), ((), ()))
contract_first = (((0,), (0,)), ((), ()))
f32 = jnp.float32
bf16 = jnp.bfloat16
vmem = pl.BlockSpec(memory_space=pltpu.VMEM)
smem = pl.BlockSpec(memory_space=pltpu.SMEM)
id_lanes = 128
costs = {
    "prep": 10,
    "pt0": 20,
    "pt1": 20,
    "pc0": 20,
    "pc1": 20,
    "pc2": 20,
    "fwd": 20,
    "bwd0": 20,
    "bwd1": 20,
    "co0": 20,
    "co1": 20,
    "co2": 20,
    "cg0": 1,
    "cg1": 1,
    "cg2": 1,
    "ddk1": 5,
    "ddk0": 5,
    "dik1": 5,
    "dik0": 5,
}
order = {
    "t3": ("t1",),
    "c2": ("t1", "t2",),
    "c3": ("t3", "yt0", "wx",),
    "c1": ("t3", "c2", "yt0",),
    "pc0": ("yt0", "pt1",),
    "wp1": ("c2", "t3",),
    "pc2": ("yt1", "yc0", "wp1", "fwd",),
    "yo0": ("yc2",),
    "co2": ("bwd1",),
    "yg1": ("yg2",),
    "yg0": ("yg2", "yo0",),
    "yo1": ("yo2",),
    "g": ("dd", "di",),
    "cg1": ("ddk0",),
    "cg0": ("dik0",),
}


def scramble(values):
    values = values ^ values >> 16 & 65535
    values = values * mixing_factor
    values = values ^ values >> 16 & 65535
    values = values * mixing_factor
    return values ^ values >> 16 & 65535


def flipped(values, axis, mask):
    return lax.ppermute(values, axis, [(i, i ^ mask) for i in range(lax.axis_size(axis))])


def after(values, *earlier):
    return lax.optimization_barrier((values,) + earlier)[0]


def called(kernel, out_shape, in_specs, cost, scratch=()):
    return pl.pallas_call(
        kernel,
        out_shape=out_shape,
        in_specs=in_specs,
        out_specs=jax.tree.map(lambda _: vmem, out_shape),
        scratch_shapes=list(scratch),
        compiler_params=pltpu.CompilerParams(vmem_limit_bytes=40 * 1024 * 1024),
        cost_estimate=pl.CostEstimate(
            flops=cost * 10**9, bytes_accessed=cost * 3 * 10**6, transcendentals=0
        ),
    )


def shape(dims, kind):
    return jax.ShapeDtypeStruct(dims, kind)


def prepare_kernel(top_count, plane_experts, capacity, place_ref, table_ref, slot_ref, gate_ref):
    planes, tok_rows = table_ref.shape[1:]
    token = lax.broadcasted_iota(jnp.int32, (tok_rows, tok_rows), 0)
    later = lax.broadcasted_iota(jnp.int32, (tok_rows, tok_rows), 1)
    earlier = jnp.where(token < later, 1.0, 0.0).astype(bf16)
    place = lax.broadcasted_iota(jnp.int32, (planes, tok_rows), 0)
    for column in range(plane_experts):
        expert = place_ref[0] ^ column
        named = jnp.zeros((planes, tok_rows), f32)
        gates = jnp.zeros((planes, tok_rows), f32)
        for k in range(top_count):
            hit = table_ref[k] == expert
            named = jnp.where(hit, 1.0, named)
            gates = jnp.where(hit, table_ref[top_count + k].astype(f32), gates)
        rank = jnp.dot(named.astype(bf16), earlier, preferred_element_type=f32).astype(jnp.int32)
        slot_ref[column] = jnp.where(named > 0.0, (place >> 1) * capacity + rank, -1)
        gate_ref[column] = gates * (1.0 / 64.0)


def choice_of(slot_ref, gate_ref, column, place, first, rows):
    row = lax.broadcasted_iota(jnp.int32, (rows, slot_ref.shape[2]), 0) + first
    hit = row == slot_ref[column, place : place + 1, :]
    if gate_ref is None:
        return jnp.where(hit, 1.0, 0.0).astype(bf16)
    return jnp.where(hit, gate_ref[column, place : place + 1, :], 0.0).astype(bf16)


def compact_kernel(places, first, with_ids, slot_ref, gate_ref, *refs):
    plane_experts, _, tok_rows = slot_ref.shape
    chunk_refs, out_refs = refs[: len(places)], refs[len(places) :]
    stacked = jnp.concatenate([chunk[...] for chunk in chunk_refs], axis=0)
    if with_ids:
        number = lax.broadcasted_iota(jnp.int32, (tok_rows, id_lanes), 0).astype(f32).astype(bf16)
        stacked = jnp.concatenate(
            [stacked, jnp.concatenate([number] * len(places), axis=0)], axis=1
        )
    for column in range(plane_experts):
        rows = out_refs[column].shape[0]
        choice = jnp.concatenate(
            [
                choice_of(slot_ref, None if with_ids else gate_ref, column, place, first, rows)
                for place in places
            ],
            axis=1,
        )
        out_refs[column][...] = jnp.dot(choice, stacked, preferred_element_type=f32).astype(bf16)


def combine_kernel(places, first, scaled, slot_ref, gate_ref, *refs):
    plane_experts = slot_ref.shape[0]
    block_refs, out_refs = refs[:plane_experts], refs[plane_experts:]
    rows = block_refs[0].shape[0]
    stacked = jnp.concatenate([block[...] for block in block_refs], axis=0)
    for place, out_ref in zip(places, out_refs):
        choice = jnp.concatenate(
            [
                choice_of(slot_ref, gate_ref if scaled else None, column, place, first, rows)
                for column in range(plane_experts)
            ],
            axis=0,
        )
        out_ref[...] = lax.dot_general(
            choice, stacked, contract_first, preferred_element_type=f32
        ).astype(out_ref.dtype)


def assemble(weight_ref, piece_refs, place_ref, seq_count):
    _, half_width, width = piece_refs[0].shape
    for index, piece in enumerate(piece_refs):
        part = lax.rem(place_ref[1] + index % seq_count, seq_count)
        column = pl.multiple_of(part * width, width)
        row = index // seq_count * half_width
        for kind in range(3):
            weight_ref[kind, row : row + half_width, pl.ds(column, width)] = piece[kind]


def stored(values, out_refs):
    start = 0
    for out in out_refs:
        out[...] = values[start : start + out.shape[0]]
        start += out.shape[0]


def forward_kernel(seq_count, plane_experts, capacity, layout, outs, place_ref, key_ref, *refs):
    row_refs, refs = refs[: len(layout)], refs[len(layout) :]
    piece_refs, refs = refs[: 2 * seq_count], refs[2 * seq_count :]
    out_refs, refs = refs[:outs], refs[outs:]
    gate_refs, up_refs, hidden_refs, weight_ref = refs[:2], refs[2:4], refs[4:6], refs[6]
    assemble(weight_ref, piece_refs, place_ref, seq_count)
    _, hidden_width, model_width = weight_ref.shape
    half_width = hidden_width // 2
    unit = lax.broadcasted_iota(jnp.int32, (1, hidden_width), 1)
    columns = place_ref[2] + jnp.where(
        unit < half_width, unit + place_ref[3], unit - half_width + place_ref[4]
    )
    spread_columns = columns * 40503
    base_hash = scramble(key_ref[0] ^ scramble(key_ref[1]))
    inputs = jnp.concatenate([row[:, :model_width] for row in row_refs], axis=0)
    gate_pre = lax.dot_general(inputs, weight_ref[0], contract_last, preferred_element_type=f32)
    up_pre = lax.dot_general(inputs, weight_ref[1], contract_last, preferred_element_type=f32)
    shift = capacity.bit_length() - 1
    mixed = []
    for (half, column, first), row in zip(layout, row_refs):
        within = row[:, model_width : model_width + id_lanes].astype(f32).astype(jnp.int32)
        step = (lax.broadcasted_iota(jnp.int32, within.shape, 0) + first) >> shift
        source = place_ref[5] ^ ((2 * step + half) * (2 * plane_experts) + 2 * column)
        ids = (place_ref[6] + source) * place_ref[7] + within
        mixed.append(scramble(ids ^ base_hash))
    mixed = jnp.concatenate(mixed, axis=0)[:, 0:1]
    hashed = scramble(mixed ^ spread_columns)
    keep = jnp.where((hashed & 1023) >= 128, f32(8.0 / 7.0), f32(0.0))
    sigmoid_gate = jax.nn.sigmoid(gate_pre)
    silu_gate = gate_pre * sigmoid_gate
    hidden = (silu_gate * up_pre * keep).astype(bf16)
    stored(up_pre * sigmoid_gate * (1.0 + gate_pre * (1.0 - sigmoid_gate)) * keep, gate_refs)
    stored(silu_gate * keep, up_refs)
    stored(hidden, hidden_refs)
    stored(jnp.dot(hidden, weight_ref[2], preferred_element_type=f32).astype(bf16), out_refs)


def backward_kernel(seq_count, blocks, outs, place_ref, *refs):
    cot_refs, refs = refs[:blocks], refs[blocks:]
    piece_refs, refs = refs[: 2 * seq_count], refs[2 * seq_count :]
    (gate_ref, up_ref), refs = refs[:2], refs[2:]
    out_refs, (gate_grad_ref, up_grad_ref, weight_ref) = refs[:outs], refs[outs:]
    assemble(weight_ref, piece_refs, place_ref, seq_count)
    cot = jnp.concatenate([block[...] for block in cot_refs], axis=0)
    hidden_grad = lax.dot_general(cot, weight_ref[2], contract_last, preferred_element_type=f32)
    gate_grad = (hidden_grad * gate_ref[...]).astype(bf16)
    up_grad = (hidden_grad * up_ref[...]).astype(bf16)
    gate_grad_ref[...] = gate_grad
    up_grad_ref[...] = up_grad
    input_grad = (
        jnp.dot(gate_grad, weight_ref[0], preferred_element_type=f32)
        + jnp.dot(up_grad, weight_ref[1], preferred_element_type=f32)
    ).astype(bf16)
    stored(input_grad, out_refs)


def weight_grad_kernel(blocks, seq_count, shift, kinds, place_ref, *refs):
    row_refs, refs = refs[:blocks], refs[blocks:]
    left_refs, refs = refs[: 2 * kinds], refs[2 * kinds :]
    added = refs[: seq_count - 1] if shift == 0 else ()
    out_refs = refs[len(added) :]
    width = out_refs[0].shape[2]
    part = lax.rem(place_ref[1] + shift, seq_count)
    lanes = pl.ds(pl.multiple_of(part * width, width), width)
    right = jnp.concatenate([row[:, lanes] for row in row_refs], axis=0)
    for kind in range(kinds):
        left = jnp.concatenate([ref[...] for ref in left_refs[2 * kind : 2 * kind + 2]], axis=0)
        total = lax.dot_general(left, right, contract_first, preferred_element_type=f32)
        for part_ref in added:
            total = total + part_ref[kind].astype(f32)
        if shift:
            out_refs[0][kind] = total.astype(bf16)
        else:
            half_width = total.shape[0] // 2
            out_refs[0][kind] = total[:half_width]
            out_refs[1][kind] = total[half_width:].astype(bf16)


def local(tokens, cotangent, routes, gate_codes, dropout_key, w_gate, w_up, w_down):
    seq_count = lax.axis_size("seq")
    block_count = lax.axis_size("blk")
    seq_index = lax.axis_index("seq")
    blk_index = lax.axis_index("blk")
    tok_rows, model_width = tokens.shape
    top_count = routes.shape[1]
    expert_count = block_count // 2
    capacity = 2 * tok_rows * top_count // expert_count
    half_width = w_gate.shape[2]
    part_width = w_gate.shape[1]
    hidden_width = 2 * half_width
    planes = 1 << (block_count.bit_length() // 2)
    plane_experts = expert_count // planes
    plane_stride = 2 * plane_experts
    parity = blk_index % 2
    expert_here = blk_index // 2
    half_rows = plane_experts * (planes // 2) * capacity
    even, odd = list(range(0, planes, 2)), list(range(1, planes, 2))
    cut = len(odd) // 2
    whole_halves, cut_halves = [even, odd], [even, odd[:cut], odd[cut:]]
    groups = {"t": whole_halves, "c": cut_halves, "o": cut_halves, "g": cut_halves}

    def group_rows(group):
        return len(group) * capacity

    def first_slot(group):
        return group[0] // 2 * capacity

    def layout(kind, halves=(0, 1)):
        return [
            (half, column, index)
            for half in halves
            for column in range(plane_experts)
            for index, group in enumerate(groups[kind])
            if group[0] % 2 == half
        ]

    place = jnp.stack(
        [
            expert_here,
            seq_index,
            expert_here * hidden_width,
            parity * half_width,
            (1 - parity) * half_width,
            blk_index,
            seq_index * block_count,
            jnp.int32(tok_rows),
        ]
    ).astype(jnp.int32)

    steps = {}
    made = {}

    def step(name, build):
        steps[name] = build

    def get(name):
        if name not in made:
            waits = [jax.tree.leaves(get(other))[0] for other in order.get(name, ())]
            with jax.named_scope(name):
                made[name] = steps[name](lambda value: after(value, *waits) if waits else value)
        return made[name]

    def across(mask):
        return lambda value: flipped(value, "blk", mask)

    def low_bit(origin):
        return origin & -origin

    def shifted(values, shift):
        return lax.ppermute(
            values, "seq", [(i, (i + shift) % seq_count) for i in range(seq_count)]
        )

    table = jnp.concatenate([routes.T, gate_codes.T], axis=0)
    for origin in range(1, planes):
        step(
            f"T{origin}",
            lambda wait, origin=origin: flipped(wait(table), "blk", origin * plane_stride),
        )

    for kind, part in (("t", tokens), ("c", cotangent)):
        step(f"{kind}0", lambda wait, part=part: part)
        for origin in range(1, planes):
            step(
                f"{kind}{origin}",
                lambda wait, kind=kind, origin=origin: flipped(
                    wait(get(f"{kind}{origin - low_bit(origin)}")),
                    "blk",
                    low_bit(origin) * plane_stride,
                ),
            )

    own_weights = jnp.stack([w_gate[0].T, w_up[0].T, w_down[0]])
    step("ow", lambda wait: own_weights)
    step("wx", lambda wait: flipped(wait(own_weights), "blk", 1))
    for shift in range(1, seq_count):
        step(f"ws{shift}", lambda wait, shift=shift: shifted(wait(own_weights), -shift))
        step(f"wp{shift}", lambda wait, shift=shift: shifted(wait(get("wx")), -shift))

    def pieces():
        others = range(1, seq_count)
        return [own_weights, *(get(f"ws{k}") for k in others)] + [
            get("wx"),
            *(get(f"wp{k}") for k in others),
        ]

    step(
        "prep",
        lambda wait: called(
            functools.partial(prepare_kernel, top_count, plane_experts, capacity),
            (
                shape((plane_experts, planes, tok_rows), jnp.int32),
                shape((plane_experts, planes, tok_rows), f32),
            ),
            [smem, vmem],
            costs["prep"],
        )(
            place,
            wait(jnp.stack([table] + [get(f"T{k}") for k in range(1, planes)], axis=1)),
        ),
    )

    def packed(kind, index, wait):
        group = groups[kind][index]
        width = model_width + (id_lanes if kind == "t" else 0)
        chunks = [get(f"{kind}{origin}") for origin in group]
        chunks[0] = wait(chunks[0])
        return called(
            functools.partial(compact_kernel, group, first_slot(group), kind == "t"),
            [shape((group_rows(group), width), bf16)] * plane_experts,
            [vmem] * (2 + len(chunks)),
            costs[f"p{kind}{index}"],
        )(*get("prep"), *chunks)

    def exchanged(by_column, wait):
        return [None] + [
            flipped(wait(by_column(column)), "blk", 2 * column)
            for column in range(1, plane_experts)
        ]

    for kind in "tc":
        for index in range(len(groups[kind])):
            step(
                f"p{kind}{index}",
                lambda wait, kind=kind, index=index: packed(kind, index, wait),
            )
            step(
                f"y{kind}{index}",
                lambda wait, kind=kind, index=index: exchanged(
                    lambda column: get(f"p{kind}{index}")[column], wait
                ),
            )

    def row_blocks(kind, halves=(0, 1)):
        return [
            get(f"{'y' if column else 'p'}{kind}{index}")[column]
            for half, column, index in layout(kind, halves)
        ]

    weight_scratch = pltpu.VMEM((3, hidden_width, model_width), bf16)

    def out_shapes(kind, halves=(0, 1)):
        return [
            shape((group_rows(groups[kind][index]), model_width), bf16)
            for half, column, index in layout(kind, halves)
        ]

    def forward(wait):
        row_parts, piece_parts = row_blocks("t"), pieces()
        row_parts[0] = wait(row_parts[0])
        described = [
            (half, column, first_slot(groups["t"][index])) for half, column, index in layout("t")
        ]
        outs = out_shapes("o")
        results = called(
            functools.partial(
                forward_kernel, seq_count, plane_experts, capacity, described, len(outs)
            ),
            outs
            + [shape((half_rows, hidden_width), f32)] * 4
            + [shape((half_rows, hidden_width), bf16)] * 2,
            [smem, smem] + [vmem] * (len(row_parts) + len(piece_parts)),
            costs["fwd"],
            [weight_scratch],
        )(place, dropout_key, *row_parts, *piece_parts)
        return results[len(outs) :] + results[: len(outs)]

    def backward(half, wait):
        cot_parts, piece_parts = row_blocks("c", (half,)), pieces()
        cot_parts[0] = wait(cot_parts[0])
        outs = out_shapes("g", (half,))
        results = called(
            functools.partial(backward_kernel, seq_count, len(cot_parts), len(outs)),
            outs + [shape((half_rows, hidden_width), bf16)] * 2,
            [smem] + [vmem] * (len(cot_parts) + len(piece_parts) + 2),
            costs[f"bwd{half}"],
            [weight_scratch],
        )(place, *cot_parts, *piece_parts, get("fwd")[half], get("fwd")[2 + half])
        return results[len(outs) :] + results[: len(outs)]

    step("fwd", forward)
    for half in (0, 1):
        step(f"bwd{half}", lambda wait, half=half: backward(half, wait))

    def slot_block(kind, column, index):
        half = groups[kind][index][0] % 2
        if kind == "o":
            return get("fwd")[6 + layout("o").index((half, column, index))]
        return get(f"bwd{half}")[2 + layout("g", (half,)).index((half, column, index))]

    def combined(kind, index, wait):
        group = groups[kind][index]
        held = [wait(slot_block(kind, 0, index)), *get(f"y{kind}{index}")[1:]]
        return called(
            functools.partial(combine_kernel, group, first_slot(group), kind == "o"),
            [shape((tok_rows, model_width), bf16 if group[0] % 2 else f32)] * len(group),
            [vmem] * (2 + plane_experts),
            costs[f"c{kind}{index}"],
        )(*get("prep"), *held)

    def total(kind, origin):
        index = [origin in group for group in groups[kind]].index(True)
        value = get(f"c{kind}{index}")[groups[kind][index].index(origin)]
        for other in range(origin + 1, planes):
            if other - low_bit(other) == origin:
                value = value.astype(f32) + get(f"z{kind}{other}").astype(f32)
        return value.astype(bf16)

    for kind in "og":
        for index in range(len(groups[kind])):
            step(
                f"y{kind}{index}",
                lambda wait, kind=kind, index=index: exchanged(
                    lambda column: slot_block(kind, column, index), wait
                ),
            )
            step(
                f"c{kind}{index}",
                lambda wait, kind=kind, index=index: combined(kind, index, wait),
            )
        for origin in range(1, planes):
            step(
                f"z{kind}{origin}",
                lambda wait, kind=kind, origin=origin: flipped(
                    wait(total(kind, origin)), "blk", low_bit(origin) * plane_stride
                ),
            )
        step(f"{kind}", lambda wait, kind=kind: wait(total(kind, 0)))

    def weight_kernel(name, wait, shift):
        if name == "dd":
            row_parts, lefts = row_blocks("c"), list(get("fwd")[4:6])
        else:
            row_parts = row_blocks("t")
            lefts = [get(f"bwd{half}")[kind] for kind in (0, 1) for half in (0, 1)]
        kinds = len(lefts) // 2
        arrived = [] if shift else [get(f"{name}s{k}") for k in range(1, seq_count)]
        lefts = [wait(lefts[0]), *lefts[1:]]
        if shift:
            result = [shape((kinds, hidden_width, part_width), bf16)]
        else:
            result = [
                shape((kinds, half_width, part_width), f32),
                shape((kinds, half_width, part_width), bf16),
            ]
        return called(
            functools.partial(weight_grad_kernel, len(row_parts), seq_count, shift, kinds),
            result,
            [smem] + [vmem] * (len(row_parts) + len(lefts) + len(arrived)),
            costs[f"{name}k{min(shift, 1)}"],
        )(place, *row_parts, *lefts, *arrived)

    for name in ("dd", "di"):
        for shift in range(seq_count):
            step(
                f"{name}k{shift}",
                lambda wait, name=name, shift=shift: weight_kernel(name, wait, shift),
            )
            step(
                f"{name}s{shift}",
                lambda wait, name=name, shift=shift: shifted(
                    wait(get(f"{name}k{shift}")[0]), shift
                ),
            )
        step(f"{name}x", lambda wait, name=name: across(1)(wait(get(f"{name}k0")[1])))
        step(
            name,
            lambda wait, name=name: [
                (wait(own) + other.astype(f32)).astype(bf16)
                for own, other in zip(get(f"{name}k0")[0], get(f"{name}x"))
            ],
        )

    down_grad, input_grads = get("dd"), get("di")
    return (
        get("o"),
        get("g"),
        input_grads[0].T[None],
        input_grads[1].T[None],
        down_grad[0][None],
    )


def solution(mesh):
    placed = (
        P(("seq", "blk"), None),
        P(("seq", "blk"), None),
        P(("seq", "blk"), None),
        P(("seq", "blk"), None),
        P(),
        P("blk", "seq", None),
        P("blk", "seq", None),
        P("blk", None, "seq"),
    )
    return jax.shard_map(
        local,
        mesh=mesh,
        in_specs=placed,
        out_specs=(
            P(("seq", "blk"), None),
            P(("seq", "blk"), None),
            P("blk", "seq", None),
            P("blk", "seq", None),
            P("blk", None, "seq"),
        ),
        check_vma=False,
    )
```

```python
import functools

import jax
import jax.numpy as jnp
from jax import lax
from jax.experimental import pallas as pl
from jax.experimental.pallas import tpu as pltpu
from jax.sharding import PartitionSpec as P

mixing_factor = 73244475
contract_last = (((1,), (1,)), ((), ()))
contract_first = (((0,), (0,)), ((), ()))
f32 = jnp.float32
bf16 = jnp.bfloat16
vmem = pl.BlockSpec(memory_space=pltpu.VMEM)
smem = pl.BlockSpec(memory_space=pltpu.SMEM)
id_lanes = 128
costs = {
    "prep": 10,
    "pt0": 20,
    "pt1": 20,
    "pc0": 20,
    "pc1": 20,
    "pc2": 20,
    "fwd": 20,
    "bwd0": 20,
    "bwd1": 20,
    "co0": 20,
    "co1": 20,
    "co2": 20,
    "cg0": 20,
    "cg1": 1,
    "cg2": 1,
    "ddk1": 5,
    "ddk0": 5,
    "dik1": 5,
    "dik0": 5,
}
order = {
    "t3": ("t1",),
    "c2": ("t1", "t2",),
    "c3": ("t3", "yt0", "wx",),
    "c1": ("t3", "c2", "yt0",),
    "pc0": ("yt0", "pt1",),
    "wp1": ("t3",),
    "pc2": ("yt1", "yc0", "wp1", "fwd",),
    "yo0": ("yc2",),
    "co2": ("bwd1",),
    "yg1": ("yg2",),
    "yg0": ("yg2", "yo0",),
    "g": ("dd", "dix",),
    "cg1": ("ddk0", "co0",),
    "cg0": ("dik0",),
    "dd": ("di",),
    "dik1": ("ddk1", "yo1",),
    "zg2": ("dik0",),
    "pt0": ("prep",),
    "dis1": ("ddk1",),
}


def scramble(values):
    values = values ^ values >> 16 & 65535
    values = values * mixing_factor
    values = values ^ values >> 16 & 65535
    values = values * mixing_factor
    return values ^ values >> 16 & 65535


def flipped(values, axis, mask):
    return lax.ppermute(values, axis, [(i, i ^ mask) for i in range(lax.axis_size(axis))])


def after(values, *earlier):
    return lax.optimization_barrier((values,) + earlier)[0]


def called(kernel, out_shape, in_specs, cost, scratch=()):
    return pl.pallas_call(
        kernel,
        out_shape=out_shape,
        in_specs=in_specs,
        out_specs=jax.tree.map(lambda _: vmem, out_shape),
        scratch_shapes=list(scratch),
        compiler_params=pltpu.CompilerParams(vmem_limit_bytes=40 * 1024 * 1024),
        cost_estimate=pl.CostEstimate(
            flops=cost * 10**9, bytes_accessed=cost * 3 * 10**6, transcendentals=0
        ),
    )


def shape(dims, kind):
    return jax.ShapeDtypeStruct(dims, kind)


def prepare_kernel(top_count, plane_experts, capacity, place_ref, table_ref, slot_ref, gate_ref):
    planes, tok_rows = table_ref.shape[1:]
    token = lax.broadcasted_iota(jnp.int32, (tok_rows, tok_rows), 0)
    later = lax.broadcasted_iota(jnp.int32, (tok_rows, tok_rows), 1)
    earlier = jnp.where(token < later, 1.0, 0.0).astype(bf16)
    place = lax.broadcasted_iota(jnp.int32, (planes, tok_rows), 0)
    for column in range(plane_experts):
        expert = place_ref[0] ^ column
        named = jnp.zeros((planes, tok_rows), f32)
        gates = jnp.zeros((planes, tok_rows), f32)
        for k in range(top_count):
            hit = table_ref[k] == expert
            named = jnp.where(hit, 1.0, named)
            gates = jnp.where(hit, table_ref[top_count + k].astype(f32), gates)
        rank = jnp.dot(named.astype(bf16), earlier, preferred_element_type=f32).astype(jnp.int32)
        slot_ref[column] = jnp.where(named > 0.0, (place >> 1) * capacity + rank, -1)
        gate_ref[column] = gates * (1.0 / 64.0)


def choice_of(slot_ref, gate_ref, column, place, first, rows):
    row = lax.broadcasted_iota(jnp.int32, (rows, slot_ref.shape[2]), 0) + first
    hit = row == slot_ref[column, place : place + 1, :]
    if gate_ref is None:
        return jnp.where(hit, 1.0, 0.0).astype(bf16)
    return jnp.where(hit, gate_ref[column, place : place + 1, :], 0.0).astype(bf16)


def compact_kernel(places, first, with_ids, slot_ref, gate_ref, *refs):
    plane_experts, _, tok_rows = slot_ref.shape
    chunk_refs, out_refs = refs[: len(places)], refs[len(places) :]
    stacked = jnp.concatenate([chunk[...] for chunk in chunk_refs], axis=0)
    if with_ids:
        number = lax.broadcasted_iota(jnp.int32, (tok_rows, id_lanes), 0).astype(f32).astype(bf16)
        stacked = jnp.concatenate(
            [stacked, jnp.concatenate([number] * len(places), axis=0)], axis=1
        )
    for column in range(plane_experts):
        rows = out_refs[column].shape[0]
        choice = jnp.concatenate(
            [
                choice_of(slot_ref, None if with_ids else gate_ref, column, place, first, rows)
                for place in places
            ],
            axis=1,
        )
        out_refs[column][...] = jnp.dot(choice, stacked, preferred_element_type=f32).astype(bf16)


def combine_kernel(places, first, scaled, slot_ref, gate_ref, *refs):
    plane_experts = slot_ref.shape[0]
    block_refs, out_refs = refs[:plane_experts], refs[plane_experts:]
    rows = block_refs[0].shape[0]
    stacked = jnp.concatenate([block[...] for block in block_refs], axis=0)
    for place, out_ref in zip(places, out_refs):
        choice = jnp.concatenate(
            [
                choice_of(slot_ref, gate_ref if scaled else None, column, place, first, rows)
                for column in range(plane_experts)
            ],
            axis=0,
        )
        out_ref[...] = lax.dot_general(
            choice, stacked, contract_first, preferred_element_type=f32
        ).astype(out_ref.dtype)


def assemble(weight_ref, piece_refs, place_ref, seq_count):
    _, half_width, width = piece_refs[0].shape
    for index, piece in enumerate(piece_refs):
        part = lax.rem(place_ref[1] + index % seq_count, seq_count)
        column = pl.multiple_of(part * width, width)
        row = index // seq_count * half_width
        for kind in range(3):
            weight_ref[kind, row : row + half_width, pl.ds(column, width)] = piece[kind]


def stored(values, out_refs):
    start = 0
    for out in out_refs:
        out[...] = values[start : start + out.shape[0]]
        start += out.shape[0]


def forward_kernel(seq_count, plane_experts, capacity, layout, outs, place_ref, key_ref, *refs):
    row_refs, refs = refs[: len(layout)], refs[len(layout) :]
    piece_refs, refs = refs[: 2 * seq_count], refs[2 * seq_count :]
    out_refs, refs = refs[:outs], refs[outs:]
    gate_refs, up_refs, hidden_refs, weight_ref = refs[:2], refs[2:4], refs[4:6], refs[6]
    assemble(weight_ref, piece_refs, place_ref, seq_count)
    _, hidden_width, model_width = weight_ref.shape
    half_width = hidden_width // 2
    unit = lax.broadcasted_iota(jnp.int32, (1, hidden_width), 1)
    columns = place_ref[2] + jnp.where(
        unit < half_width, unit + place_ref[3], unit - half_width + place_ref[4]
    )
    spread_columns = columns * 40503
    base_hash = scramble(key_ref[0] ^ scramble(key_ref[1]))
    inputs = jnp.concatenate([row[:, :model_width] for row in row_refs], axis=0)
    gate_pre = lax.dot_general(inputs, weight_ref[0], contract_last, preferred_element_type=f32)
    up_pre = lax.dot_general(inputs, weight_ref[1], contract_last, preferred_element_type=f32)
    shift = capacity.bit_length() - 1
    mixed = []
    for (half, column, first), row in zip(layout, row_refs):
        within = row[:, model_width : model_width + id_lanes].astype(f32).astype(jnp.int32)
        step = (lax.broadcasted_iota(jnp.int32, within.shape, 0) + first) >> shift
        source = place_ref[5] ^ ((2 * step + half) * (2 * plane_experts) + 2 * column)
        ids = (place_ref[6] + source) * place_ref[7] + within
        mixed.append(scramble(ids ^ base_hash))
    mixed = jnp.concatenate(mixed, axis=0)[:, 0:1]
    hashed = scramble(mixed ^ spread_columns)
    keep = jnp.where((hashed & 1023) >= 128, f32(8.0 / 7.0), f32(0.0))
    sigmoid_gate = jax.nn.sigmoid(gate_pre)
    silu_gate = gate_pre * sigmoid_gate
    hidden = (silu_gate * up_pre * keep).astype(bf16)
    stored(up_pre * sigmoid_gate * (1.0 + gate_pre * (1.0 - sigmoid_gate)) * keep, gate_refs)
    stored(silu_gate * keep, up_refs)
    stored(hidden, hidden_refs)
    stored(jnp.dot(hidden, weight_ref[2], preferred_element_type=f32).astype(bf16), out_refs)


def backward_kernel(seq_count, blocks, outs, place_ref, *refs):
    cot_refs, refs = refs[:blocks], refs[blocks:]
    piece_refs, refs = refs[: 2 * seq_count], refs[2 * seq_count :]
    (gate_ref, up_ref), refs = refs[:2], refs[2:]
    out_refs, (gate_grad_ref, up_grad_ref, weight_ref) = refs[:outs], refs[outs:]
    assemble(weight_ref, piece_refs, place_ref, seq_count)
    cot = jnp.concatenate([block[...] for block in cot_refs], axis=0)
    hidden_grad = lax.dot_general(cot, weight_ref[2], contract_last, preferred_element_type=f32)
    gate_grad = (hidden_grad * gate_ref[...]).astype(bf16)
    up_grad = (hidden_grad * up_ref[...]).astype(bf16)
    gate_grad_ref[...] = gate_grad
    up_grad_ref[...] = up_grad
    input_grad = (
        jnp.dot(gate_grad, weight_ref[0], preferred_element_type=f32)
        + jnp.dot(up_grad, weight_ref[1], preferred_element_type=f32)
    ).astype(bf16)
    stored(input_grad, out_refs)


def weight_grad_kernel(blocks, seq_count, shift, kinds, place_ref, *refs):
    row_refs, refs = refs[:blocks], refs[blocks:]
    left_refs, refs = refs[: 2 * kinds], refs[2 * kinds :]
    added = refs[: seq_count - 1] if shift == 0 else ()
    out_refs = refs[len(added) :]
    width = out_refs[0].shape[2]
    part = lax.rem(place_ref[1] + shift, seq_count)
    lanes = pl.ds(pl.multiple_of(part * width, width), width)
    right = jnp.concatenate([row[:, lanes] for row in row_refs], axis=0)
    for kind in range(kinds):
        left = jnp.concatenate([ref[...] for ref in left_refs[2 * kind : 2 * kind + 2]], axis=0)
        total = lax.dot_general(left, right, contract_first, preferred_element_type=f32)
        for part_ref in added:
            total = total + part_ref[kind].astype(f32)
        if shift:
            out_refs[0][kind] = total.astype(bf16)
        else:
            half_width = total.shape[0] // 2
            out_refs[0][kind] = total[:half_width]
            out_refs[1][kind] = total[half_width:].astype(bf16)


def local(tokens, cotangent, routes, gate_codes, dropout_key, w_gate, w_up, w_down):
    seq_count = lax.axis_size("seq")
    block_count = lax.axis_size("blk")
    seq_index = lax.axis_index("seq")
    blk_index = lax.axis_index("blk")
    tok_rows, model_width = tokens.shape
    top_count = routes.shape[1]
    expert_count = block_count // 2
    capacity = 2 * tok_rows * top_count // expert_count
    half_width = w_gate.shape[2]
    part_width = w_gate.shape[1]
    hidden_width = 2 * half_width
    planes = 1 << (block_count.bit_length() // 2)
    plane_experts = expert_count // planes
    plane_stride = 2 * plane_experts
    parity = blk_index % 2
    expert_here = blk_index // 2
    half_rows = plane_experts * (planes // 2) * capacity
    even, odd = list(range(0, planes, 2)), list(range(1, planes, 2))
    cut = len(odd) // 2
    whole_halves, cut_halves = [even, odd], [even, odd[:cut], odd[cut:]]
    groups = {"t": whole_halves, "c": cut_halves, "o": cut_halves, "g": cut_halves}

    def group_rows(group):
        return len(group) * capacity

    def first_slot(group):
        return group[0] // 2 * capacity

    def layout(kind, halves=(0, 1)):
        return [
            (half, column, index)
            for half in halves
            for column in range(plane_experts)
            for index, group in enumerate(groups[kind])
            if group[0] % 2 == half
        ]

    place = jnp.stack(
        [
            expert_here,
            seq_index,
            expert_here * hidden_width,
            parity * half_width,
            (1 - parity) * half_width,
            blk_index,
            seq_index * block_count,
            jnp.int32(tok_rows),
        ]
    ).astype(jnp.int32)

    steps = {}
    made = {}

    def step(name, build):
        steps[name] = build

    def get(name):
        if name not in made:
            waits = [jax.tree.leaves(get(other))[0] for other in order.get(name, ())]
            with jax.named_scope(name):
                made[name] = steps[name](lambda value: after(value, *waits) if waits else value)
        return made[name]

    def across(mask):
        return lambda value: flipped(value, "blk", mask)

    def low_bit(origin):
        return origin & -origin

    def shifted(values, shift):
        return lax.ppermute(
            values, "seq", [(i, (i + shift) % seq_count) for i in range(seq_count)]
        )

    table = jnp.concatenate([routes.T, gate_codes.T], axis=0)
    for origin in range(1, planes):
        step(
            f"T{origin}",
            lambda wait, origin=origin: flipped(wait(table), "blk", origin * plane_stride),
        )

    for kind, part in (("t", tokens), ("c", cotangent)):
        step(f"{kind}0", lambda wait, part=part: part)
        for origin in range(1, planes):
            step(
                f"{kind}{origin}",
                lambda wait, kind=kind, origin=origin: flipped(
                    wait(get(f"{kind}{origin - low_bit(origin)}")),
                    "blk",
                    low_bit(origin) * plane_stride,
                ),
            )

    own_weights = jnp.stack([w_gate[0].T, w_up[0].T, w_down[0]])
    step("ow", lambda wait: own_weights)
    step("wx", lambda wait: flipped(wait(own_weights), "blk", 1))
    for shift in range(1, seq_count):
        step(f"ws{shift}", lambda wait, shift=shift: shifted(wait(own_weights), -shift))
        step(f"wp{shift}", lambda wait, shift=shift: shifted(wait(get("wx")), -shift))

    def pieces():
        others = range(1, seq_count)
        return [own_weights, *(get(f"ws{k}") for k in others)] + [
            get("wx"),
            *(get(f"wp{k}") for k in others),
        ]

    step(
        "prep",
        lambda wait: called(
            functools.partial(prepare_kernel, top_count, plane_experts, capacity),
            (
                shape((plane_experts, planes, tok_rows), jnp.int32),
                shape((plane_experts, planes, tok_rows), f32),
            ),
            [smem, vmem],
            costs["prep"],
        )(
            place,
            wait(jnp.stack([table] + [get(f"T{k}") for k in range(1, planes)], axis=1)),
        ),
    )

    def packed(kind, index, wait):
        group = groups[kind][index]
        width = model_width + (id_lanes if kind == "t" else 0)
        chunks = [get(f"{kind}{origin}") for origin in group]
        chunks[0] = wait(chunks[0])
        return called(
            functools.partial(compact_kernel, group, first_slot(group), kind == "t"),
            [shape((group_rows(group), width), bf16)] * plane_experts,
            [vmem] * (2 + len(chunks)),
            costs[f"p{kind}{index}"],
        )(*get("prep"), *chunks)

    def exchanged(by_column, wait):
        return [None] + [
            flipped(wait(by_column(column)), "blk", 2 * column)
            for column in range(1, plane_experts)
        ]

    for kind in "tc":
        for index in range(len(groups[kind])):
            step(
                f"p{kind}{index}",
                lambda wait, kind=kind, index=index: packed(kind, index, wait),
            )
            step(
                f"y{kind}{index}",
                lambda wait, kind=kind, index=index: exchanged(
                    lambda column: get(f"p{kind}{index}")[column], wait
                ),
            )

    def row_blocks(kind, halves=(0, 1)):
        return [
            get(f"{'y' if column else 'p'}{kind}{index}")[column]
            for half, column, index in layout(kind, halves)
        ]

    weight_scratch = pltpu.VMEM((3, hidden_width, model_width), bf16)

    def out_shapes(kind, halves=(0, 1)):
        return [
            shape((group_rows(groups[kind][index]), model_width), bf16)
            for half, column, index in layout(kind, halves)
        ]

    def forward(wait):
        row_parts, piece_parts = row_blocks("t"), pieces()
        row_parts[0] = wait(row_parts[0])
        described = [
            (half, column, first_slot(groups["t"][index])) for half, column, index in layout("t")
        ]
        outs = out_shapes("o")
        results = called(
            functools.partial(
                forward_kernel, seq_count, plane_experts, capacity, described, len(outs)
            ),
            outs
            + [shape((half_rows, hidden_width), f32)] * 4
            + [shape((half_rows, hidden_width), bf16)] * 2,
            [smem, smem] + [vmem] * (len(row_parts) + len(piece_parts)),
            costs["fwd"],
            [weight_scratch],
        )(place, dropout_key, *row_parts, *piece_parts)
        return results[len(outs) :] + results[: len(outs)]

    def backward(half, wait):
        cot_parts, piece_parts = row_blocks("c", (half,)), pieces()
        cot_parts[0] = wait(cot_parts[0])
        outs = out_shapes("g", (half,))
        results = called(
            functools.partial(backward_kernel, seq_count, len(cot_parts), len(outs)),
            outs + [shape((half_rows, hidden_width), bf16)] * 2,
            [smem] + [vmem] * (len(cot_parts) + len(piece_parts) + 2),
            costs[f"bwd{half}"],
            [weight_scratch],
        )(place, *cot_parts, *piece_parts, get("fwd")[half], get("fwd")[2 + half])
        return results[len(outs) :] + results[: len(outs)]

    step("fwd", forward)
    for half in (0, 1):
        step(f"bwd{half}", lambda wait, half=half: backward(half, wait))

    def slot_block(kind, column, index):
        half = groups[kind][index][0] % 2
        if kind == "o":
            return get("fwd")[6 + layout("o").index((half, column, index))]
        return get(f"bwd{half}")[2 + layout("g", (half,)).index((half, column, index))]

    def combined(kind, index, wait):
        group = groups[kind][index]
        held = [wait(slot_block(kind, 0, index)), *get(f"y{kind}{index}")[1:]]
        return called(
            functools.partial(combine_kernel, group, first_slot(group), kind == "o"),
            [shape((tok_rows, model_width), bf16 if group[0] % 2 else f32)] * len(group),
            [vmem] * (2 + plane_experts),
            costs[f"c{kind}{index}"],
        )(*get("prep"), *held)

    def total(kind, origin):
        index = [origin in group for group in groups[kind]].index(True)
        value = get(f"c{kind}{index}")[groups[kind][index].index(origin)]
        for other in range(origin + 1, planes):
            if other - low_bit(other) == origin:
                value = value.astype(f32) + get(f"z{kind}{other}").astype(f32)
        return value.astype(bf16)

    for kind in "og":
        for index in range(len(groups[kind])):
            step(
                f"y{kind}{index}",
                lambda wait, kind=kind, index=index: exchanged(
                    lambda column: slot_block(kind, column, index), wait
                ),
            )
            step(
                f"c{kind}{index}",
                lambda wait, kind=kind, index=index: combined(kind, index, wait),
            )
        for origin in range(1, planes):
            step(
                f"z{kind}{origin}",
                lambda wait, kind=kind, origin=origin: flipped(
                    wait(total(kind, origin)), "blk", low_bit(origin) * plane_stride
                ),
            )
        step(f"{kind}", lambda wait, kind=kind: wait(total(kind, 0)))

    def weight_kernel(name, wait, shift):
        if name == "dd":
            row_parts, lefts = row_blocks("c"), list(get("fwd")[4:6])
        else:
            row_parts = row_blocks("t")
            lefts = [get(f"bwd{half}")[kind] for kind in (0, 1) for half in (0, 1)]
        kinds = len(lefts) // 2
        arrived = [] if shift else [get(f"{name}s{k}") for k in range(1, seq_count)]
        lefts = [wait(lefts[0]), *lefts[1:]]
        if shift:
            result = [shape((kinds, hidden_width, part_width), bf16)]
        else:
            result = [
                shape((kinds, half_width, part_width), f32),
                shape((kinds, half_width, part_width), bf16),
            ]
        return called(
            functools.partial(weight_grad_kernel, len(row_parts), seq_count, shift, kinds),
            result,
            [smem] + [vmem] * (len(row_parts) + len(lefts) + len(arrived)),
            costs[f"{name}k{min(shift, 1)}"],
        )(place, *row_parts, *lefts, *arrived)

    for name in ("dd", "di"):
        for shift in range(seq_count):
            step(
                f"{name}k{shift}",
                lambda wait, name=name, shift=shift: weight_kernel(name, wait, shift),
            )
            step(
                f"{name}s{shift}",
                lambda wait, name=name, shift=shift: shifted(
                    wait(get(f"{name}k{shift}")[0]), shift
                ),
            )
        step(f"{name}x", lambda wait, name=name: across(1)(wait(get(f"{name}k0")[1])))
        step(
            name,
            lambda wait, name=name: [
                (wait(own) + other.astype(f32)).astype(bf16)
                for own, other in zip(get(f"{name}k0")[0], get(f"{name}x"))
            ],
        )

    down_grad, input_grads = get("dd"), get("di")
    return (
        get("o"),
        get("g"),
        input_grads[0].T[None],
        input_grads[1].T[None],
        down_grad[0][None],
    )


def solution(mesh):
    placed = (
        P(("seq", "blk"), None),
        P(("seq", "blk"), None),
        P(("seq", "blk"), None),
        P(("seq", "blk"), None),
        P(),
        P("blk", "seq", None),
        P("blk", "seq", None),
        P("blk", None, "seq"),
    )
    return jax.shard_map(
        local,
        mesh=mesh,
        in_specs=placed,
        out_specs=(
            P(("seq", "blk"), None),
            P(("seq", "blk"), None),
            P("blk", "seq", None),
            P("blk", "seq", None),
            P("blk", None, "seq"),
        ),
        check_vma=False,
    )
```

```python
import functools

import jax
import jax.numpy as jnp
from jax import lax
from jax.experimental import pallas as pl
from jax.experimental.pallas import tpu as pltpu
from jax.sharding import PartitionSpec as P

mixing_factor = 73244475
contract_last = (((1,), (1,)), ((), ()))
contract_first = (((0,), (0,)), ((), ()))
f32 = jnp.float32
bf16 = jnp.bfloat16
vmem = pl.BlockSpec(memory_space=pltpu.VMEM)
smem = pl.BlockSpec(memory_space=pltpu.SMEM)
id_lanes = 128
costs = {
    "prep": 10,
    "pt0": 5,
    "pt1": 20,
    "pc0": 20,
    "pc1": 20,
    "pc2": 20,
    "fwd": 20,
    "bwd0": 20,
    "bwd1": 20,
    "co0": 20,
    "co1": 20,
    "co2": 20,
    "cg0": 20,
    "cg1": 1,
    "cg2": 1,
    "ddk1": 5,
    "ddk0": 5,
    "dik1": 5,
    "dik0": 5,
}
order = {
    "t3": ("t1",),
    "c2": ("t1", "t2",),
    "c3": ("t3", "yt0", "wx",),
    "c1": ("t3", "c2", "yt0",),
    "pc0": ("yt0", "pt1",),
    "wp1": ("t3",),
    "pc2": ("yt1", "yc0", "wp1", "fwd",),
    "yo0": ("yc2",),
    "co2": ("bwd1",),
    "yg1": ("yg2",),
    "yg0": ("yg2", "yo0", "dis1",),
    "g": ("dix",),
    "cg1": ("ddk0", "co0",),
    "cg0": ("dik0",),
    "dd": ("di",),
    "dik1": ("ddk1", "yo1",),
    "zg2": ("dik0",),
    "pt0": ("prep",),
    "dis1": ("ddk1",),
    "pc1": ("wp1",),
}


def scramble(values):
    values = values ^ values >> 16 & 65535
    values = values * mixing_factor
    values = values ^ values >> 16 & 65535
    values = values * mixing_factor
    return values ^ values >> 16 & 65535


def flipped(values, axis, mask):
    return lax.ppermute(values, axis, [(i, i ^ mask) for i in range(lax.axis_size(axis))])


def after(values, *earlier):
    return lax.optimization_barrier((values,) + earlier)[0]


def called(kernel, out_shape, in_specs, cost, scratch=()):
    return pl.pallas_call(
        kernel,
        out_shape=out_shape,
        in_specs=in_specs,
        out_specs=jax.tree.map(lambda _: vmem, out_shape),
        scratch_shapes=list(scratch),
        compiler_params=pltpu.CompilerParams(vmem_limit_bytes=40 * 1024 * 1024),
        cost_estimate=pl.CostEstimate(
            flops=cost * 10**9, bytes_accessed=cost * 3 * 10**6, transcendentals=0
        ),
    )


def shape(dims, kind):
    return jax.ShapeDtypeStruct(dims, kind)


def prepare_kernel(top_count, plane_experts, capacity, place_ref, table_ref, slot_ref, gate_ref):
    planes, tok_rows = table_ref.shape[1:]
    token = lax.broadcasted_iota(jnp.int32, (tok_rows, tok_rows), 0)
    later = lax.broadcasted_iota(jnp.int32, (tok_rows, tok_rows), 1)
    earlier = jnp.where(token < later, 1.0, 0.0).astype(bf16)
    place = lax.broadcasted_iota(jnp.int32, (planes, tok_rows), 0)
    for column in range(plane_experts):
        expert = place_ref[0] ^ column
        named = jnp.zeros((planes, tok_rows), f32)
        gates = jnp.zeros((planes, tok_rows), f32)
        for k in range(top_count):
            hit = table_ref[k] == expert
            named = jnp.where(hit, 1.0, named)
            gates = jnp.where(hit, table_ref[top_count + k].astype(f32), gates)
        rank = jnp.dot(named.astype(bf16), earlier, preferred_element_type=f32).astype(jnp.int32)
        slot_ref[column] = jnp.where(named > 0.0, (place >> 1) * capacity + rank, -1)
        gate_ref[column] = gates * (1.0 / 64.0)


def choice_of(slot_ref, gate_ref, column, place, first, rows):
    row = lax.broadcasted_iota(jnp.int32, (rows, slot_ref.shape[2]), 0) + first
    hit = row == slot_ref[column, place : place + 1, :]
    if gate_ref is None:
        return jnp.where(hit, 1.0, 0.0).astype(bf16)
    return jnp.where(hit, gate_ref[column, place : place + 1, :], 0.0).astype(bf16)


def compact_kernel(places, first, with_ids, slot_ref, gate_ref, *refs):
    plane_experts, _, tok_rows = slot_ref.shape
    chunk_refs, out_refs = refs[: len(places)], refs[len(places) :]
    stacked = jnp.concatenate([chunk[...] for chunk in chunk_refs], axis=0)
    if with_ids:
        number = lax.broadcasted_iota(jnp.int32, (tok_rows, id_lanes), 0).astype(f32).astype(bf16)
        stacked = jnp.concatenate(
            [stacked, jnp.concatenate([number] * len(places), axis=0)], axis=1
        )
    for column in range(plane_experts):
        rows = out_refs[column].shape[0]
        choice = jnp.concatenate(
            [
                choice_of(slot_ref, None if with_ids else gate_ref, column, place, first, rows)
                for place in places
            ],
            axis=1,
        )
        out_refs[column][...] = jnp.dot(choice, stacked, preferred_element_type=f32).astype(bf16)


def combine_kernel(places, first, scaled, slot_ref, gate_ref, *refs):
    plane_experts = slot_ref.shape[0]
    block_refs, out_refs = refs[:plane_experts], refs[plane_experts:]
    rows = block_refs[0].shape[0]
    stacked = jnp.concatenate([block[...] for block in block_refs], axis=0)
    for place, out_ref in zip(places, out_refs):
        choice = jnp.concatenate(
            [
                choice_of(slot_ref, gate_ref if scaled else None, column, place, first, rows)
                for column in range(plane_experts)
            ],
            axis=0,
        )
        out_ref[...] = lax.dot_general(
            choice, stacked, contract_first, preferred_element_type=f32
        ).astype(out_ref.dtype)


def assemble(weight_ref, piece_refs, place_ref, seq_count):
    _, half_width, width = piece_refs[0].shape
    for index, piece in enumerate(piece_refs):
        part = lax.rem(place_ref[1] + index % seq_count, seq_count)
        column = pl.multiple_of(part * width, width)
        row = index // seq_count * half_width
        for kind in range(3):
            weight_ref[kind, row : row + half_width, pl.ds(column, width)] = piece[kind]


def stored(values, out_refs):
    start = 0
    for out in out_refs:
        out[...] = values[start : start + out.shape[0]]
        start += out.shape[0]


def forward_kernel(seq_count, plane_experts, capacity, layout, outs, place_ref, key_ref, *refs):
    row_refs, refs = refs[: len(layout)], refs[len(layout) :]
    piece_refs, refs = refs[: 2 * seq_count], refs[2 * seq_count :]
    out_refs, refs = refs[:outs], refs[outs:]
    gate_refs, up_refs, hidden_refs, weight_ref = refs[:2], refs[2:4], refs[4:6], refs[6]
    assemble(weight_ref, piece_refs, place_ref, seq_count)
    _, hidden_width, model_width = weight_ref.shape
    half_width = hidden_width // 2
    unit = lax.broadcasted_iota(jnp.int32, (1, hidden_width), 1)
    columns = place_ref[2] + jnp.where(
        unit < half_width, unit + place_ref[3], unit - half_width + place_ref[4]
    )
    spread_columns = columns * 40503
    base_hash = scramble(key_ref[0] ^ scramble(key_ref[1]))
    inputs = jnp.concatenate([row[:, :model_width] for row in row_refs], axis=0)
    gate_pre = lax.dot_general(inputs, weight_ref[0], contract_last, preferred_element_type=f32)
    up_pre = lax.dot_general(inputs, weight_ref[1], contract_last, preferred_element_type=f32)
    shift = capacity.bit_length() - 1
    mixed = []
    for (half, column, first), row in zip(layout, row_refs):
        within = row[:, model_width : model_width + id_lanes].astype(f32).astype(jnp.int32)
        step = (lax.broadcasted_iota(jnp.int32, within.shape, 0) + first) >> shift
        source = place_ref[5] ^ ((2 * step + half) * (2 * plane_experts) + 2 * column)
        ids = (place_ref[6] + source) * place_ref[7] + within
        mixed.append(scramble(ids ^ base_hash))
    mixed = jnp.concatenate(mixed, axis=0)[:, 0:1]
    hashed = scramble(mixed ^ spread_columns)
    keep = jnp.where((hashed & 1023) >= 128, f32(8.0 / 7.0), f32(0.0))
    sigmoid_gate = jax.nn.sigmoid(gate_pre)
    silu_gate = gate_pre * sigmoid_gate
    hidden = (silu_gate * up_pre * keep).astype(bf16)
    stored(up_pre * sigmoid_gate * (1.0 + gate_pre * (1.0 - sigmoid_gate)) * keep, gate_refs)
    stored(silu_gate * keep, up_refs)
    stored(hidden, hidden_refs)
    stored(jnp.dot(hidden, weight_ref[2], preferred_element_type=f32).astype(bf16), out_refs)


def backward_kernel(seq_count, blocks, outs, place_ref, *refs):
    cot_refs, refs = refs[:blocks], refs[blocks:]
    piece_refs, refs = refs[: 2 * seq_count], refs[2 * seq_count :]
    (gate_ref, up_ref), refs = refs[:2], refs[2:]
    out_refs, (gate_grad_ref, up_grad_ref, weight_ref) = refs[:outs], refs[outs:]
    assemble(weight_ref, piece_refs, place_ref, seq_count)
    cot = jnp.concatenate([block[...] for block in cot_refs], axis=0)
    hidden_grad = lax.dot_general(cot, weight_ref[2], contract_last, preferred_element_type=f32)
    gate_grad = (hidden_grad * gate_ref[...]).astype(bf16)
    up_grad = (hidden_grad * up_ref[...]).astype(bf16)
    gate_grad_ref[...] = gate_grad
    up_grad_ref[...] = up_grad
    input_grad = (
        jnp.dot(gate_grad, weight_ref[0], preferred_element_type=f32)
        + jnp.dot(up_grad, weight_ref[1], preferred_element_type=f32)
    ).astype(bf16)
    stored(input_grad, out_refs)


def weight_grad_kernel(blocks, seq_count, shift, kinds, place_ref, *refs):
    row_refs, refs = refs[:blocks], refs[blocks:]
    left_refs, refs = refs[: 2 * kinds], refs[2 * kinds :]
    added = refs[: seq_count - 1] if shift == 0 else ()
    out_refs = refs[len(added) :]
    width = out_refs[0].shape[2]
    part = lax.rem(place_ref[1] + shift, seq_count)
    lanes = pl.ds(pl.multiple_of(part * width, width), width)
    right = jnp.concatenate([row[:, lanes] for row in row_refs], axis=0)
    for kind in range(kinds):
        left = jnp.concatenate([ref[...] for ref in left_refs[2 * kind : 2 * kind + 2]], axis=0)
        total = lax.dot_general(left, right, contract_first, preferred_element_type=f32)
        for part_ref in added:
            total = total + part_ref[kind].astype(f32)
        if shift:
            out_refs[0][kind] = total.astype(bf16)
        else:
            half_width = total.shape[0] // 2
            out_refs[0][kind] = total[:half_width]
            out_refs[1][kind] = total[half_width:].astype(bf16)


def local(tokens, cotangent, routes, gate_codes, dropout_key, w_gate, w_up, w_down):
    seq_count = lax.axis_size("seq")
    block_count = lax.axis_size("blk")
    seq_index = lax.axis_index("seq")
    blk_index = lax.axis_index("blk")
    tok_rows, model_width = tokens.shape
    top_count = routes.shape[1]
    expert_count = block_count // 2
    capacity = 2 * tok_rows * top_count // expert_count
    half_width = w_gate.shape[2]
    part_width = w_gate.shape[1]
    hidden_width = 2 * half_width
    planes = 1 << (block_count.bit_length() // 2)
    plane_experts = expert_count // planes
    plane_stride = 2 * plane_experts
    parity = blk_index % 2
    expert_here = blk_index // 2
    half_rows = plane_experts * (planes // 2) * capacity
    even, odd = list(range(0, planes, 2)), list(range(1, planes, 2))
    cut = len(odd) // 2
    whole_halves, cut_halves = [even, odd], [even, odd[:cut], odd[cut:]]
    groups = {"t": whole_halves, "c": cut_halves, "o": cut_halves, "g": cut_halves}

    def group_rows(group):
        return len(group) * capacity

    def first_slot(group):
        return group[0] // 2 * capacity

    def layout(kind, halves=(0, 1)):
        return [
            (half, column, index)
            for half in halves
            for column in range(plane_experts)
            for index, group in enumerate(groups[kind])
            if group[0] % 2 == half
        ]

    place = jnp.stack(
        [
            expert_here,
            seq_index,
            expert_here * hidden_width,
            parity * half_width,
            (1 - parity) * half_width,
            blk_index,
            seq_index * block_count,
            jnp.int32(tok_rows),
        ]
    ).astype(jnp.int32)

    steps = {}
    made = {}

    def step(name, build):
        steps[name] = build

    def get(name):
        if name not in made:
            waits = [jax.tree.leaves(get(other))[0] for other in order.get(name, ())]
            with jax.named_scope(name):
                made[name] = steps[name](lambda value: after(value, *waits) if waits else value)
        return made[name]

    def across(mask):
        return lambda value: flipped(value, "blk", mask)

    def low_bit(origin):
        return origin & -origin

    def shifted(values, shift):
        return lax.ppermute(
            values, "seq", [(i, (i + shift) % seq_count) for i in range(seq_count)]
        )

    table = jnp.concatenate([routes.T, gate_codes.T], axis=0)
    for origin in range(1, planes):
        step(
            f"T{origin}",
            lambda wait, origin=origin: flipped(wait(table), "blk", origin * plane_stride),
        )

    for kind, part in (("t", tokens), ("c", cotangent)):
        step(f"{kind}0", lambda wait, part=part: part)
        for origin in range(1, planes):
            step(
                f"{kind}{origin}",
                lambda wait, kind=kind, origin=origin: flipped(
                    wait(get(f"{kind}{origin - low_bit(origin)}")),
                    "blk",
                    low_bit(origin) * plane_stride,
                ),
            )

    own_weights = jnp.stack([w_gate[0].T, w_up[0].T, w_down[0]])
    step("ow", lambda wait: own_weights)
    step("wx", lambda wait: flipped(wait(own_weights), "blk", 1))
    for shift in range(1, seq_count):
        step(f"ws{shift}", lambda wait, shift=shift: shifted(wait(own_weights), -shift))
        step(f"wp{shift}", lambda wait, shift=shift: shifted(wait(get("wx")), -shift))

    def pieces():
        others = range(1, seq_count)
        return [own_weights, *(get(f"ws{k}") for k in others)] + [
            get("wx"),
            *(get(f"wp{k}") for k in others),
        ]

    step(
        "prep",
        lambda wait: called(
            functools.partial(prepare_kernel, top_count, plane_experts, capacity),
            (
                shape((plane_experts, planes, tok_rows), jnp.int32),
                shape((plane_experts, planes, tok_rows), f32),
            ),
            [smem, vmem],
            costs["prep"],
        )(
            place,
            wait(jnp.stack([table] + [get(f"T{k}") for k in range(1, planes)], axis=1)),
        ),
    )

    def packed(kind, index, wait):
        group = groups[kind][index]
        width = model_width + (id_lanes if kind == "t" else 0)
        chunks = [get(f"{kind}{origin}") for origin in group]
        chunks[0] = wait(chunks[0])
        return called(
            functools.partial(compact_kernel, group, first_slot(group), kind == "t"),
            [shape((group_rows(group), width), bf16)] * plane_experts,
            [vmem] * (2 + len(chunks)),
            costs[f"p{kind}{index}"],
        )(*get("prep"), *chunks)

    def exchanged(by_column, wait):
        return [None] + [
            flipped(wait(by_column(column)), "blk", 2 * column)
            for column in range(1, plane_experts)
        ]

    for kind in "tc":
        for index in range(len(groups[kind])):
            step(
                f"p{kind}{index}",
                lambda wait, kind=kind, index=index: packed(kind, index, wait),
            )
            step(
                f"y{kind}{index}",
                lambda wait, kind=kind, index=index: exchanged(
                    lambda column: get(f"p{kind}{index}")[column], wait
                ),
            )

    def row_blocks(kind, halves=(0, 1)):
        return [
            get(f"{'y' if column else 'p'}{kind}{index}")[column]
            for half, column, index in layout(kind, halves)
        ]

    weight_scratch = pltpu.VMEM((3, hidden_width, model_width), bf16)

    def out_shapes(kind, halves=(0, 1)):
        return [
            shape((group_rows(groups[kind][index]), model_width), bf16)
            for half, column, index in layout(kind, halves)
        ]

    def forward(wait):
        row_parts, piece_parts = row_blocks("t"), pieces()
        row_parts[0] = wait(row_parts[0])
        described = [
            (half, column, first_slot(groups["t"][index])) for half, column, index in layout("t")
        ]
        outs = out_shapes("o")
        results = called(
            functools.partial(
                forward_kernel, seq_count, plane_experts, capacity, described, len(outs)
            ),
            outs
            + [shape((half_rows, hidden_width), f32)] * 4
            + [shape((half_rows, hidden_width), bf16)] * 2,
            [smem, smem] + [vmem] * (len(row_parts) + len(piece_parts)),
            costs["fwd"],
            [weight_scratch],
        )(place, dropout_key, *row_parts, *piece_parts)
        return results[len(outs) :] + results[: len(outs)]

    def backward(half, wait):
        cot_parts, piece_parts = row_blocks("c", (half,)), pieces()
        cot_parts[0] = wait(cot_parts[0])
        outs = out_shapes("g", (half,))
        results = called(
            functools.partial(backward_kernel, seq_count, len(cot_parts), len(outs)),
            outs + [shape((half_rows, hidden_width), bf16)] * 2,
            [smem] + [vmem] * (len(cot_parts) + len(piece_parts) + 2),
            costs[f"bwd{half}"],
            [weight_scratch],
        )(place, *cot_parts, *piece_parts, get("fwd")[half], get("fwd")[2 + half])
        return results[len(outs) :] + results[: len(outs)]

    step("fwd", forward)
    for half in (0, 1):
        step(f"bwd{half}", lambda wait, half=half: backward(half, wait))

    def slot_block(kind, column, index):
        half = groups[kind][index][0] % 2
        if kind == "o":
            return get("fwd")[6 + layout("o").index((half, column, index))]
        return get(f"bwd{half}")[2 + layout("g", (half,)).index((half, column, index))]

    def combined(kind, index, wait):
        group = groups[kind][index]
        held = [wait(slot_block(kind, 0, index)), *get(f"y{kind}{index}")[1:]]
        return called(
            functools.partial(combine_kernel, group, first_slot(group), kind == "o"),
            [shape((tok_rows, model_width), bf16 if group[0] % 2 else f32)] * len(group),
            [vmem] * (2 + plane_experts),
            costs[f"c{kind}{index}"],
        )(*get("prep"), *held)

    def total(kind, origin):
        index = [origin in group for group in groups[kind]].index(True)
        value = get(f"c{kind}{index}")[groups[kind][index].index(origin)]
        for other in range(origin + 1, planes):
            if other - low_bit(other) == origin:
                value = value.astype(f32) + get(f"z{kind}{other}").astype(f32)
        return value.astype(bf16)

    for kind in "og":
        for index in range(len(groups[kind])):
            step(
                f"y{kind}{index}",
                lambda wait, kind=kind, index=index: exchanged(
                    lambda column: slot_block(kind, column, index), wait
                ),
            )
            step(
                f"c{kind}{index}",
                lambda wait, kind=kind, index=index: combined(kind, index, wait),
            )
        for origin in range(1, planes):
            step(
                f"z{kind}{origin}",
                lambda wait, kind=kind, origin=origin: flipped(
                    wait(total(kind, origin)), "blk", low_bit(origin) * plane_stride
                ),
            )
        step(f"{kind}", lambda wait, kind=kind: wait(total(kind, 0)))

    def weight_kernel(name, wait, shift):
        if name == "dd":
            row_parts, lefts = row_blocks("c"), list(get("fwd")[4:6])
        else:
            row_parts = row_blocks("t")
            lefts = [get(f"bwd{half}")[kind] for kind in (0, 1) for half in (0, 1)]
        kinds = len(lefts) // 2
        arrived = [] if shift else [get(f"{name}s{k}") for k in range(1, seq_count)]
        lefts = [wait(lefts[0]), *lefts[1:]]
        if shift:
            result = [shape((kinds, hidden_width, part_width), bf16)]
        else:
            result = [
                shape((kinds, half_width, part_width), f32),
                shape((kinds, half_width, part_width), bf16),
            ]
        return called(
            functools.partial(weight_grad_kernel, len(row_parts), seq_count, shift, kinds),
            result,
            [smem] + [vmem] * (len(row_parts) + len(lefts) + len(arrived)),
            costs[f"{name}k{min(shift, 1)}"],
        )(place, *row_parts, *lefts, *arrived)

    for name in ("dd", "di"):
        for shift in range(seq_count):
            step(
                f"{name}k{shift}",
                lambda wait, name=name, shift=shift: weight_kernel(name, wait, shift),
            )
            step(
                f"{name}s{shift}",
                lambda wait, name=name, shift=shift: shifted(
                    wait(get(f"{name}k{shift}")[0]), shift
                ),
            )
        step(f"{name}x", lambda wait, name=name: across(1)(wait(get(f"{name}k0")[1])))
        step(
            name,
            lambda wait, name=name: [
                (wait(own) + other.astype(f32)).astype(bf16)
                for own, other in zip(get(f"{name}k0")[0], get(f"{name}x"))
            ],
        )

    down_grad, input_grads = get("dd"), get("di")
    return (
        get("o"),
        get("g"),
        input_grads[0].T[None],
        input_grads[1].T[None],
        down_grad[0][None],
    )


def solution(mesh):
    placed = (
        P(("seq", "blk"), None),
        P(("seq", "blk"), None),
        P(("seq", "blk"), None),
        P(("seq", "blk"), None),
        P(),
        P("blk", "seq", None),
        P("blk", "seq", None),
        P("blk", None, "seq"),
    )
    return jax.shard_map(
        local,
        mesh=mesh,
        in_specs=placed,
        out_specs=(
            P(("seq", "blk"), None),
            P(("seq", "blk"), None),
            P("blk", "seq", None),
            P("blk", "seq", None),
            P("blk", None, "seq"),
        ),
        check_vma=False,
    )
```
